128 devices in a mesh: group: 8 (over z, y_hi), member: 16 (over y_lo, x, core).
Axes of the slice: x: 4, y: 4 (y_hi: 2, y_lo: 2; y = y_hi * 2 + y_lo), z: 4, core: 2. Of those that a mesh axis runs over, the one named last changes fastest.
Arguments:
- raw_strain: float32 [5120, 4160], P(('group', 'member')), may hold values from -6 to 6
- fir_taps: float32 [64], replicated, may hold values from -0.75 to 0.75
- block_slot: int32 [5120], P(('group', 'member')), may hold values from 0 to 39, as said below
- pairings: int32 [2, 8], P(None, 'group'), may hold values from 0 to 7, as said below
- pair_subset: int32 [2, 16, 1], P(None, 'member'), may hold values from 0 to 15, as said below
Outputs:
- correlations: bfloat16 [2, 1, 5120, 40, 2048], P(None, None, ('group', 'member'))
The draws below stay inside these ranges and needn't reach their ends.
Inputs may be any that keep to these rules, and one draw needn't show every extreme that they name: `block_slot`: the 40 entries of each block are a permutation of 0 to 39. Each row pairs the groups: pairings[r, pairings[r, g]] = g and pairings[r, g] != g; the rows are different rounds of one round-robin tournament. `pair_subset`: in each round, each member's 1 entries are different, and each member index is named by exactly 1 of the 16 rows.
All inputs are finite; a program needn't handle non-finite values.
Results may differ from the reference program's by a relative error of at most 0.006.
Values may be sent and summed in bfloat16 or wider, within the bound.
A program may use at most 128 MiB of HBM per device.

```python
import math
import jax
import jax.numpy as jnp
from jax import lax

CH = 40
SEG = 2048
TAPS = 64
NFFT = 4096
F0 = 24
NBIN = 1024
WIN = 64
LAG = 1024
ROUNDS = 2
KSUB = 1
RAW = 4160
CHANNELS = 5120
N_GROUP = 8
N_MEMBER = 16


def draw_block_slot(key, part):
    key = jax.random.fold_in(key, 29)
    block_keys = jax.random.split(key, N_GROUP * N_MEMBER)

    def shuffle_block(block_key):
        return jax.random.permutation(block_key, CH)
    return jax.vmap(shuffle_block)(block_keys).reshape(-1).astype(jnp.int32)


def draw_pairings(key, part):
    key = jax.random.fold_in(key, 17)
    label_key, round_key = jax.random.split(key)
    labels = jax.random.permutation(label_key, N_GROUP).astype(jnp.int32)
    picks = jax.random.permutation(round_key, N_GROUP - 1)[:ROUNDS].astype(jnp.int32)
    teams = jnp.arange(N_GROUP, dtype=jnp.int32)

    def one_round(pick):
        partner_raw = jnp.mod(2 * pick - teams, N_GROUP - 1)
        partner_raw = jnp.where(partner_raw == teams, N_GROUP - 1, partner_raw)
        partner_raw = jnp.where(teams == N_GROUP - 1, pick, partner_raw)
        return jnp.zeros((N_GROUP,), jnp.int32).at[labels].set(labels[partner_raw])
    return jax.vmap(one_round)(picks).astype(jnp.int32)


def draw_pair_subset(key, part):
    key = jax.random.fold_in(key, 23)
    round_keys = jax.random.split(key, ROUNDS)

    def one_round(round_key):
        order_key, offset_key = jax.random.split(round_key)
        member_order = jax.random.permutation(order_key, N_MEMBER).astype(jnp.int32)
        offsets = jnp.concatenate([jnp.zeros((1,), jnp.int32), jax.random.permutation(offset_key, N_MEMBER - 1)[:KSUB - 1].astype(jnp.int32) + 1])
        positions = jnp.mod(jnp.arange(N_MEMBER, dtype=jnp.int32)[:, None] + offsets[None, :], N_MEMBER)
        return member_order[positions]
    return jax.vmap(one_round)(round_keys).astype(jnp.int32)


def levels(rng, shape, cuts, least, top_value):
    factor_of, own = 1.0, jax.random.fold_in(rng, 6)
    for axis_at, shards_of in cuts:
        draws = jnp.exp(jax.random.uniform(jax.random.fold_in(own, axis_at), (shards_of,), jnp.float32, least / len(cuts), top_value / len(cuts)))
        factor_of = factor_of * jnp.repeat(draws, shape[axis_at] // shards_of).reshape([-1 if axis == axis_at else 1 for axis in range(len(shape))])
    return factor_of


def centred(stream_key, extent, scale, limit, cuts=(), kind=jnp.bfloat16):
    drawn = jax.random.normal(stream_key, extent, jnp.float32) * scale
    if len(cuts) > 0:
        drawn = levels(stream_key, extent, cuts, -0.22, 0.18) * drawn
    return jnp.clip(drawn, min=-limit, max=limit).astype(kind)


def setup_inputs(seed: int = 0) -> dict:
    splits = jax.random.split(jax.random.key(seed), 6)
    return {
        "raw_strain": centred(splits[0], (CHANNELS, RAW), 1.0, 6.0, ((0, 128),), jnp.float32),
        "fir_taps": centred(splits[1], (TAPS,), TAPS ** -0.5, 0.75, (), jnp.float32),
        "block_slot": draw_block_slot(jax.random.fold_in(splits[5], 71), 0),
        "pairings": draw_pairings(jax.random.fold_in(splits[5], 71), 0),
        "pair_subset": draw_pair_subset(jax.random.fold_in(splits[5], 71), 0),
    }


EPS = 1e-06
TWO_PI = 2.0 * math.pi

def decimate(raw_strain, fir_taps):
    filtered = jnp.zeros((raw_strain.shape[0], SEG), jnp.float32)
    for tap_index in range(TAPS):
        filtered = filtered + fir_taps[tap_index] * raw_strain[:, tap_index:tap_index + 2 * SEG - 1:2]
    return filtered

def forward_table():
    samples = jnp.arange(SEG, dtype=jnp.int32)
    freq_bins = F0 + jnp.arange(NBIN, dtype=jnp.int32)
    phases = jnp.mod(samples[:, None] * freq_bins[None, :], NFFT).astype(jnp.float32) * (TWO_PI / NFFT)
    return jnp.concatenate([jnp.cos(phases), -jnp.sin(phases)], axis=1)

def window_matrix():
    freq_bins = jnp.arange(NBIN, dtype=jnp.int32)
    window_start = jnp.clip(freq_bins - WIN // 2, 0, NBIN - WIN)
    inside = (freq_bins[:, None] >= window_start[None, :]) & (freq_bins[:, None] < window_start[None, :] + WIN)
    return inside.astype(jnp.float32) / WIN

def whiten(ordered):
    spectrum = jnp.dot(ordered, forward_table(), precision=lax.Precision.HIGHEST, preferred_element_type=jnp.float32)
    real_part = spectrum[:, :NBIN]
    imag_part = spectrum[:, NBIN:]
    band_power = jnp.dot(real_part * real_part + imag_part * imag_part, window_matrix(), precision=lax.Precision.HIGHEST, preferred_element_type=jnp.float32)
    inverse_amp = lax.rsqrt(band_power + EPS)
    return jnp.concatenate([real_part * inverse_amp, imag_part * inverse_amp], axis=1).astype(jnp.bfloat16)

def lag_table():
    freq_bins = F0 + jnp.arange(NBIN, dtype=jnp.int32)
    lag_values = jnp.arange(2 * LAG, dtype=jnp.int32) - LAG
    phases = jnp.mod(freq_bins[:, None] * lag_values[None, :], NFFT).astype(jnp.float32) * (TWO_PI / NFFT)
    weights = jnp.concatenate([jnp.cos(phases), -jnp.sin(phases)], axis=0) / math.sqrt(NBIN)
    return weights.astype(jnp.bfloat16)

def cross_spectra(own_panel, theirs):
    own_wide = own_panel.astype(jnp.float32)
    their_wide = theirs.astype(jnp.float32)
    a_real = own_wide[:, :NBIN][None, None, :, None, :]
    a_imag = own_wide[:, NBIN:][None, None, :, None, :]
    b_real = their_wide[..., :NBIN][:, :, None, :, :]
    b_imag = their_wide[..., NBIN:][:, :, None, :, :]
    c_real = a_real * b_real + a_imag * b_imag
    c_imag = a_imag * b_real - a_real * b_imag
    return jnp.concatenate([c_real, c_imag], axis=-1).astype(jnp.bfloat16).reshape(-1, 2 * NBIN)

def reference(raw_strain, fir_taps, block_slot, pairings, pair_subset):
    decimated = decimate(raw_strain, fir_taps)
    target_rows = jnp.arange(CHANNELS, dtype=jnp.int32) // CH * CH + block_slot
    ordered = jnp.zeros_like(decimated).at[target_rows].set(decimated)
    panels = whiten(ordered)
    weights = lag_table().astype(jnp.float32)

    def correlate_block(block_index):
        group_index = block_index // N_MEMBER
        member_index = block_index % N_MEMBER
        own_panel = lax.dynamic_slice_in_dim(panels, (block_index * CH).astype(jnp.int32), CH, 0)
        picked = []
        for turn_index in range(ROUNDS):
            for slot_index in range(KSUB):
                partner_block = pairings[turn_index, group_index] * N_MEMBER + pair_subset[turn_index, member_index, slot_index]
                picked.append(lax.dynamic_slice_in_dim(panels, (partner_block * CH).astype(jnp.int32), CH, 0))
        theirs = jnp.stack(picked).reshape(ROUNDS, KSUB, CH, 2 * NBIN)
        spectra_rows = cross_spectra(own_panel, theirs).astype(jnp.float32)
        result = jnp.dot(spectra_rows, weights, precision=lax.Precision.HIGHEST, preferred_element_type=jnp.float32)
        return result.astype(jnp.bfloat16).reshape(ROUNDS, KSUB, CH, CH, 2 * LAG)
    stacked = lax.map(correlate_block, jnp.arange(N_GROUP * N_MEMBER, dtype=jnp.int32))
    return jnp.transpose(stacked, (1, 2, 0, 3, 4, 5)).reshape(ROUNDS, KSUB, CHANNELS, CH, 2 * LAG)
```

```python
import functools
import math

import jax
import jax.numpy as jnp
import ml_dtypes
import numpy as np
from jax import lax
from jax.experimental import pallas as pl
from jax.experimental.pallas import tpu as pltpu
from jax.sharding import PartitionSpec as P

SEG = 2048
TAPS = 64
NFFT = 4096
F0 = 24
NBIN = 1024
WIN = 64
LAG = 1024
ROUNDS = 2
KSUB = 1
CH = 40
RAW = 4160
EPS = 1e-06

PIECE = 256
PIECES = SEG // PIECE
SPAN = 640
OWN_STEP = 8
MIB = 1 << 20
BF16 = jnp.bfloat16
F32 = jnp.float32


def split_bf16(table):
    high = table.astype(ml_dtypes.bfloat16)
    low = (table - high.astype(np.float64)).astype(ml_dtypes.bfloat16)
    return high, low


def forward_tables():
    bins = F0 + np.arange(NBIN)
    phases = np.arange(PIECE)[:, None] * bins[None, :] % NFFT * (2.0 * math.pi / NFFT)
    high, low = split_bf16(np.concatenate([np.cos(phases), -np.sin(phases)], axis=1))
    shift = np.arange(PIECES)[:, None] * PIECE * bins[None, :] % NFFT * (2.0 * math.pi / NFFT)
    return high, low, np.cos(shift).astype(np.float32), -np.sin(shift).astype(np.float32)


def lag_tables():
    bins = F0 + np.arange(NBIN)
    phases = bins[:, None] * (2 * np.arange(LAG) + 1)[None, :] % (2 * NFFT) * (math.pi / NFFT)
    scale = 1.0 / math.sqrt(NBIN)
    cosine = (np.cos(phases) * scale).astype(ml_dtypes.bfloat16)
    sine = (-np.sin(phases) * scale).astype(ml_dtypes.bfloat16)
    half = bins * (math.pi / NFFT)
    turn = np.stack([np.cos(half), -np.sin(half)]).astype(np.float32)
    flip = np.eye(256)[::-1].astype(ml_dtypes.bfloat16)
    return cosine, sine, turn, flip


def dot(a, b):
    return jnp.dot(a, b, preferred_element_type=F32)


def parts(x):
    high = x.astype(BF16)
    return high, (x - high.astype(F32)).astype(BF16)


def whiten_kernel(raw_ref, taps_ref, slot_ref, high_ref, low_ref, tc_ref, ts_ref, panel_ref, dh_ref, dl_ref, re_ref, im_ref):
    taps = jnp.concatenate([taps_ref[...], jnp.zeros((1, SPAN - 128), F32)], axis=1)
    filter_rows = pltpu.roll(jnp.broadcast_to(taps, (PIECE, SPAN)), 0, 1, stride=2, stride_axis=0)
    pieces = [raw_ref[:, 2 * PIECE * b : 2 * PIECE * b + SPAN] for b in range(PIECES - 1)]
    last = raw_ref[:, 2 * PIECE * (PIECES - 1) :]
    pieces.append(jnp.concatenate([last, jnp.zeros((CH, SPAN - last.shape[1]), F32)], axis=1))
    xh, xl = parts(jnp.concatenate(pieces, axis=0))
    fh, fl = parts(filter_rows)
    contract = functools.partial(
        lax.dot_general, dimension_numbers=(((1,), (1,)), ((), ())), preferred_element_type=F32
    )
    dh, dl = parts(contract(xh, fh) + contract(xl, fh) + contract(xh, fl))
    dh_ref[...] = dh
    dl_ref[...] = dl
    width = 256
    for n in range(NBIN // width):
        cols = slice(width * n, width * (n + 1))
        both = []
        for base in (0, NBIN):
            at = slice(base + width * n, base + width * (n + 1))
            wide = dh_ref[...]
            both.append(dot(wide, high_ref[:, at]) + dot(dl_ref[...], high_ref[:, at]) + dot(wide, low_ref[:, at]))
        yr, yi = both
        re = jnp.zeros((CH, width), F32)
        im = jnp.zeros((CH, width), F32)
        for b in range(PIECES):
            tc = tc_ref[b : b + 1, cols]
            ts = ts_ref[b : b + 1, cols]
            r, i = yr[CH * b : CH * (b + 1)], yi[CH * b : CH * (b + 1)]
            re += r * tc - i * ts
            im += r * ts + i * tc
        re_ref[:, cols] = re
        im_ref[:, cols] = im
    re, im = re_ref[...], im_ref[...]
    total = re * re + im * im
    for step in (1, 2, 4, 8, 16, 32):
        total = total + pltpu.roll(total, NBIN - step, 1)
    total = pltpu.roll(total, WIN // 2, 1)
    col = lax.broadcasted_iota(jnp.int32, (CH, NBIN), 1)
    first, final = WIN // 2, NBIN - WIN // 2
    total = jnp.where(col < first, total[:, first : first + 1], total)
    total = jnp.where(col > final, total[:, final : final + 1], total)
    inverse = lax.rsqrt(total * (1.0 / WIN) + EPS)
    place = (lax.broadcasted_iota(jnp.int32, (CH, CH), 0) == slot_ref[...]).astype(F32).astype(BF16)
    panel_ref[:, :NBIN] = dot(place, (re * inverse).astype(BF16)).astype(BF16)
    panel_ref[:, NBIN:] = dot(place, (im * inverse).astype(BF16)).astype(BF16)


def correlate_kernel(own_ref, their_ref, cos_ref, sin_ref, turn_ref, flip_ref, out_ref, cre_ref, cim_ref):
    br = their_ref[0, :, :NBIN].astype(F32)
    bi = their_ref[0, :, NBIN:].astype(F32)
    tr, ti = turn_ref[0:1, :], turn_ref[1:2, :]
    own = own_ref[...].astype(F32)
    ar0, ai0 = own[:, :NBIN], own[:, NBIN:]
    ar = ar0 * tr - ai0 * ti
    ai = ar0 * ti + ai0 * tr
    for i in range(0, OWN_STEP, 2):
        res, ims = [], []
        for k in (i, i + 1):
            r, m = ar[k : k + 1], ai[k : k + 1]
            res.append(r * br + m * bi)
            ims.append(m * br - r * bi)
        rows = slice(CH * i, CH * (i + 2))
        cre_ref[rows, :] = jnp.concatenate(res, axis=0).astype(BF16)
        cim_ref[rows, :] = jnp.concatenate(ims, axis=0).astype(BF16)
    width = 256
    for n in range(LAG // width):
        cols = slice(width * n, width * (n + 1))
        even = dot(cre_ref[...], cos_ref[:, cols])
        odd = dot(cim_ref[...], sin_ref[:, cols])
        out_ref[:, LAG + width * n : LAG + width * (n + 1)] = (even + odd).astype(BF16)
        mirrored = dot((even - odd).astype(BF16), flip_ref[...])
        out_ref[:, LAG - width * (n + 1) : LAG - width * n] = mirrored.astype(BF16)


def whiten(raw_strain, fir_taps, block_slot):
    high, low, tc, ts = forward_tables()
    taps = jnp.pad(fir_taps, (0, 128 - TAPS)).reshape(1, 128)
    return pl.pallas_call(
        whiten_kernel,
        out_shape=jax.ShapeDtypeStruct((CH, 2 * NBIN), BF16),
        in_specs=[pl.BlockSpec(memory_space=pltpu.VMEM)] * 7,
        out_specs=pl.BlockSpec(memory_space=pltpu.VMEM),
        scratch_shapes=[pltpu.VMEM((PIECES * CH, PIECE), BF16)] * 2 + [pltpu.VMEM((CH, NBIN), F32)] * 2,
        compiler_params=pltpu.CompilerParams(vmem_limit_bytes=48 * MIB),
    )(raw_strain, taps, block_slot.reshape(1, CH), high, low, tc, ts)


def correlate(own, theirs):
    cosine, sine, turn, flip = lag_tables()
    rows = OWN_STEP * CH
    steps = CH // OWN_STEP
    whole = lambda r, i: (0, 0)
    return pl.pallas_call(
        correlate_kernel,
        grid=(ROUNDS, steps),
        out_shape=jax.ShapeDtypeStruct((ROUNDS * CH * CH, 2 * LAG), BF16),
        in_specs=[
            pl.BlockSpec((OWN_STEP, 2 * NBIN), lambda r, i: (i, 0)),
            pl.BlockSpec((1, CH, 2 * NBIN), lambda r, i: (r, 0, 0)),
            pl.BlockSpec((NBIN, LAG), whole),
            pl.BlockSpec((NBIN, LAG), whole),
            pl.BlockSpec((2, NBIN), whole),
            pl.BlockSpec((256, 256), whole),
        ],
        out_specs=pl.BlockSpec((rows, 2 * LAG), lambda r, i: (r * steps + i, 0)),
        scratch_shapes=[pltpu.VMEM((rows, NBIN), BF16)] * 2,
        compiler_params=pltpu.CompilerParams(vmem_limit_bytes=48 * MIB),
    )(own, theirs, cosine, sine, turn, flip)


def per_device(raw_strain, fir_taps, block_slot, pairings, pair_subset):
    panel = whiten(raw_strain, fir_taps, block_slot)
    mine = lax.all_gather(panel, "member", axis=0)
    picked = jnp.stack(
        [lax.dynamic_index_in_dim(mine, pair_subset[r, 0, 0], 0, keepdims=False) for r in range(ROUNDS)]
    )
    around = lax.all_gather(picked, "group", axis=0)
    theirs = jnp.stack(
        [lax.dynamic_index_in_dim(around, pairings[r, 0], 0, keepdims=False)[r] for r in range(ROUNDS)]
    )
    result = correlate(panel, theirs)
    return result.reshape(ROUNDS, KSUB, CH, CH, 2 * LAG)


def solution(mesh):
    in_specs = (
        P(("group", "member"), None),
        P(),
        P(("group", "member")),
        P(None, "group"),
        P(None, "member", None),
    )
    out_specs = P(None, None, ("group", "member"), None, None)
    return jax.shard_map(
        per_device, mesh=mesh, in_specs=in_specs, out_specs=out_specs, check_vma=False
    )
```

```python
import functools
import math

import jax
import jax.numpy as jnp
import ml_dtypes
import numpy as np
from jax import lax
from jax.experimental import pallas as pl
from jax.experimental.pallas import tpu as pltpu
from jax.sharding import PartitionSpec as P

SEG = 2048
TAPS = 64
NFFT = 4096
F0 = 24
NBIN = 1024
WIN = 64
LAG = 1024
ROUNDS = 2
KSUB = 1
CH = 40
RAW = 4160
EPS = 1e-06

PIECE = 256
PIECES = SEG // PIECE
SPAN = 640
OWN_STEP = 8
MIB = 1 << 20
BF16 = jnp.bfloat16
F32 = jnp.float32


def split_bf16(table):
    high = table.astype(ml_dtypes.bfloat16)
    low = (table - high.astype(np.float64)).astype(ml_dtypes.bfloat16)
    return high, low


def forward_tables():
    bins = F0 + np.arange(NBIN)
    phases = np.arange(PIECE)[:, None] * bins[None, :] % NFFT * (2.0 * math.pi / NFFT)
    high, low = split_bf16(np.concatenate([np.cos(phases), -np.sin(phases)], axis=1))
    shift = np.arange(PIECES)[:, None] * PIECE * bins[None, :] % NFFT * (2.0 * math.pi / NFFT)
    return high, low, np.cos(shift).astype(np.float32), -np.sin(shift).astype(np.float32)


def lag_tables():
    bins = F0 + np.arange(NBIN)
    phases = bins[:, None] * (2 * np.arange(LAG) + 1)[None, :] % (2 * NFFT) * (math.pi / NFFT)
    scale = 1.0 / math.sqrt(NBIN)
    cosine = (np.cos(phases) * scale).astype(ml_dtypes.bfloat16)
    sine = (-np.sin(phases) * scale).astype(ml_dtypes.bfloat16)
    half = bins * (math.pi / NFFT)
    turn = np.stack([np.cos(half), -np.sin(half)]).astype(np.float32)
    flip = np.eye(256)[::-1].astype(ml_dtypes.bfloat16)
    return cosine, sine, turn, flip


def dot(a, b):
    return jnp.dot(a, b, preferred_element_type=F32)


def parts(x):
    high = x.astype(BF16)
    return high, (x - high.astype(F32)).astype(BF16)


def whiten_kernel(raw_ref, taps_ref, slot_ref, high_ref, low_ref, tc_ref, ts_ref, panel_ref, dh_ref, dl_ref, re_ref, im_ref):
    taps = jnp.concatenate([taps_ref[...], jnp.zeros((1, SPAN - 128), F32)], axis=1)
    filter_rows = pltpu.roll(jnp.broadcast_to(taps, (PIECE, SPAN)), 0, 1, stride=2, stride_axis=0)
    pieces = [raw_ref[:, 2 * PIECE * b : 2 * PIECE * b + SPAN] for b in range(PIECES - 1)]
    last = raw_ref[:, 2 * PIECE * (PIECES - 1) :]
    pieces.append(jnp.concatenate([last, jnp.zeros((CH, SPAN - last.shape[1]), F32)], axis=1))
    xh, xl = parts(jnp.concatenate(pieces, axis=0))
    fh, fl = parts(filter_rows)
    contract = functools.partial(
        lax.dot_general, dimension_numbers=(((1,), (1,)), ((), ())), preferred_element_type=F32
    )
    dh, dl = parts(contract(xh, fh) + contract(xl, fh) + contract(xh, fl))
    dh_ref[...] = dh
    dl_ref[...] = dl
    width = 256
    for n in range(NBIN // width):
        cols = slice(width * n, width * (n + 1))
        both = []
        for base in (0, NBIN):
            at = slice(base + width * n, base + width * (n + 1))
            wide = dh_ref[...]
            both.append(dot(wide, high_ref[:, at]) + dot(dl_ref[...], high_ref[:, at]) + dot(wide, low_ref[:, at]))
        yr, yi = both
        re = jnp.zeros((CH, width), F32)
        im = jnp.zeros((CH, width), F32)
        for b in range(PIECES):
            tc = tc_ref[b : b + 1, cols]
            ts = ts_ref[b : b + 1, cols]
            r, i = yr[CH * b : CH * (b + 1)], yi[CH * b : CH * (b + 1)]
            re += r * tc - i * ts
            im += r * ts + i * tc
        re_ref[:, cols] = re
        im_ref[:, cols] = im
    re, im = re_ref[...], im_ref[...]
    total = re * re + im * im
    for step in (1, 2, 4, 8, 16, 32):
        total = total + pltpu.roll(total, NBIN - step, 1)
    total = pltpu.roll(total, WIN // 2, 1)
    col = lax.broadcasted_iota(jnp.int32, (CH, NBIN), 1)
    first, final = WIN // 2, NBIN - WIN // 2
    total = jnp.where(col < first, total[:, first : first + 1], total)
    total = jnp.where(col > final, total[:, final : final + 1], total)
    inverse = lax.rsqrt(total * (1.0 / WIN) + EPS)
    place = (lax.broadcasted_iota(jnp.int32, (CH, CH), 0) == slot_ref[...]).astype(F32).astype(BF16)
    re = dot(place, (re * inverse).astype(BF16))
    im = dot(place, (im * inverse).astype(BF16))
    for n in range(2):
        cols = slice(HALF * n, HALF * (n + 1))
        panel_ref[n] = jnp.concatenate([re[:, cols], im[:, cols]], axis=0).astype(BF16)


def whole_bins(panel):
    wide = panel.astype(F32)
    return (
        jnp.concatenate([wide[0, :CH], wide[1, :CH]], axis=1),
        jnp.concatenate([wide[0, CH:], wide[1, CH:]], axis=1),
    )


def correlate_kernel(own_ref, their_ref, cos_ref, sin_ref, turn_ref, flip_ref, out_ref, turned_ref, cre_ref, cim_ref):
    @pl.when((pl.program_id(0) == 0) & (pl.program_id(1) == 0))
    def _():
        own_re, own_im = whole_bins(own_ref[...])
        tr, ti = turn_ref[0:1, :], turn_ref[1:2, :]
        turned_ref[0] = own_re * tr - own_im * ti
        turned_ref[1] = own_re * ti + own_im * tr

    br, bi = whole_bins(their_ref[0])
    at = pl.ds(pl.multiple_of(pl.program_id(1) * OWN_STEP, OWN_STEP), OWN_STEP)
    ar, ai = turned_ref[0, at, :], turned_ref[1, at, :]
    for i in range(0, OWN_STEP, 2):
        res, ims = [], []
        for k in (i, i + 1):
            r, m = ar[k : k + 1], ai[k : k + 1]
            res.append(r * br + m * bi)
            ims.append(m * br - r * bi)
        rows = slice(CH * i, CH * (i + 2))
        cre_ref[rows, :] = jnp.concatenate(res, axis=0).astype(BF16)
        cim_ref[rows, :] = jnp.concatenate(ims, axis=0).astype(BF16)
    width = 256
    for n in range(LAG // width):
        cols = slice(width * n, width * (n + 1))
        even = dot(cre_ref[...], cos_ref[:, cols])
        odd = dot(cim_ref[...], sin_ref[:, cols])
        out_ref[:, LAG + width * n : LAG + width * (n + 1)] = (even + odd).astype(BF16)
        mirrored = dot((even - odd).astype(BF16), flip_ref[...])
        out_ref[:, LAG - width * (n + 1) : LAG - width * n] = mirrored.astype(BF16)


HALF = NBIN // 2
MESH_ID = pl.DeviceIdType.MESH


def choose(first, a, b):
    return jnp.where(first, a.astype(F32), b.astype(F32)).astype(BF16)


def exchange_kernel(pairings_ref, subset_ref, panel_ref, theirs_ref, meta, peers, flat, row, rows0, rows1, line, lines0, lines1,
                    row_in, rows_in, line_in, lines_in, row_out, rows_out, line_out, lines_out, send, recv, local):
    g, m = lax.axis_index("group"), lax.axis_index("member")
    z, h = g // 2, g % 2
    l, x, c = m // 8, (m // 2) % 4, m % 2
    k = x * 2 + c

    def at(dz=0, dh=0, dl=0, dx=0, dc=0):
        group = lax.rem(z + dz, 4) * 2 + lax.rem(h + dh, 2)
        member = lax.rem(l + dl, 2) * 8 + lax.rem(x + dx, 4) * 2 + lax.rem(c + dc, 2)
        return group, member

    along_x = [at(dx=d) for d in (1, 3, 2)]
    along_z = [at(dz=d) for d in (1, 3, 2)]
    core, low, high = at(dc=1), at(dl=1), at(dh=1)
    started = []

    def put(src, dst, where):
        n = len(started)
        copy = pltpu.make_async_remote_copy(
            src_ref=src, dst_ref=dst, send_sem=send.at[n], recv_sem=recv.at[n], device_id=where, device_id_type=MESH_ID
        )
        copy.start()
        started.append(copy)
        return copy

    index = lax.broadcasted_iota(jnp.int32, (8, 128), 0)
    mine = jnp.zeros((8, 128), jnp.int32)
    for r in range(ROUNDS):
        mine = jnp.where(index == r, pairings_ref[r, 0], mine)
        mine = jnp.where(index == ROUNDS + r, subset_ref[r, 0], mine)
    meta[...] = mine

    barrier = pltpu.get_barrier_semaphore()
    everyone = along_x + along_z + [core, low, high]
    for where in everyone:
        pl.semaphore_signal(barrier, inc=1, device_id=where, device_id_type=MESH_ID)
    pl.semaphore_wait(barrier, len(everyone))

    asks = [put(meta, peers.at[0], low), put(meta, peers.at[1], high)]
    row[k] = panel_ref[0]
    line[z] = panel_ref[1]
    row_x = [put(panel_ref.at[0], row.at[k], where) for where in along_x]
    line_z = [put(panel_ref.at[1], line.at[z], where) for where in along_z]
    row_c = [put(panel_ref.at[0], row.at[k], core)]
    for ask in asks:
        ask.wait_recv()
    fetch = pltpu.make_async_copy(peers, flat, local)
    fetch.start()
    fetch.wait()
    my_pair = [pairings_ref[r, 0] for r in range(ROUNDS)]
    my_sub = [subset_ref[r, 0] for r in range(ROUNDS)]
    low_sub = [flat[0, ROUNDS + r, 0] for r in range(ROUNDS)]
    high_pair = [flat[1, r, 0] for r in range(ROUNDS)]

    def slot(dx):
        return lax.rem(x + dx, 4) * 2 + c

    for copy, dx in zip(row_x, (3, 1, 2)):
        copy.wait_recv()
        row_c.append(put(row.at[slot(dx)], row.at[slot(dx)], core))
    for copy in line_z:
        copy.wait_recv()
    rows, lines = (rows0, rows1), (lines0, lines1)
    in_group = [lax.rem(my_pair[r], 2) == h for r in range(ROUNDS)]
    in_member = [my_sub[r] // 8 == l for r in range(ROUNDS)]
    my_z = [my_pair[r] // 2 for r in range(ROUNDS)]
    my_k = [lax.rem(my_sub[r], 8) for r in range(ROUNDS)]
    line_y = []
    for r in range(ROUNDS):
        line_out[r] = line[high_pair[r] // 2]
        line_y.append(put(line_out.at[r], line_in.at[r], high))
    for copy in row_c:
        copy.wait_recv()
    row_y = []
    for r in range(ROUNDS):
        row_out[r] = row[lax.rem(low_sub[r], 8)]
        row_y.append(put(row_out.at[r], row_in.at[r], low))

    rows_x, rows_c, lines_z = [], [], []
    for r in range(ROUNDS):
        line_y[r].wait_recv()
        rows[r][k] = choose(in_group[r], line[my_z[r]], line_in[r])
        own = rows[r].at[k]
        rows_x.append([put(own, own, where) for where in along_x])
        rows_c.append([put(own, own, core)])
        row_y[r].wait_recv()
        lines[r][z] = choose(in_member[r], row[my_k[r]], row_in[r])
        own = lines[r].at[z]
        lines_z.append([put(own, own, where) for where in along_z])
    last_line, last_row = [], []
    for r in range(ROUNDS):
        for copy, dx in zip(rows_x[r], (3, 1, 2)):
            copy.wait_recv()
            got = rows[r].at[slot(dx)]
            rows_c[r].append(put(got, got, core))
        for copy in lines_z[r]:
            copy.wait_recv()
        lines_out[r] = lines[r][high_pair[r] // 2]
        last_line.append(put(lines_out.at[r], lines_in.at[r], high))
        for copy in rows_c[r]:
            copy.wait_recv()
        rows_out[r] = rows[r][lax.rem(low_sub[r], 8)]
        last_row.append(put(rows_out.at[r], rows_in.at[r], low))
    for r in range(ROUNDS):
        last_line[r].wait_recv()
        theirs_ref[r, 0] = choose(in_group[r], lines[r][my_z[r]], lines_in[r])
        last_row[r].wait_recv()
        theirs_ref[r, 1] = choose(in_member[r], rows[r][my_k[r]], rows_in[r])
    for copy in started:
        copy.wait_send()


COPIES = 2 + 7 + 3 + 2 + 2 + 14 + 6 + 2 + 2


def exchange(panel, pairings, subset):
    half = (2 * CH, HALF)
    return pl.pallas_call(
        exchange_kernel,
        out_shape=jax.ShapeDtypeStruct((ROUNDS, 2) + half, BF16),
        in_specs=[pl.BlockSpec(memory_space=pltpu.SMEM)] * 2 + [pl.BlockSpec(memory_space=pltpu.VMEM)],
        out_specs=pl.BlockSpec(memory_space=pltpu.VMEM),
        scratch_shapes=[
            pltpu.VMEM((8, 128), jnp.int32),
            pltpu.VMEM((2, 8, 128), jnp.int32),
            pltpu.SMEM((2, 8, 128), jnp.int32),
            pltpu.VMEM((8,) + half, BF16),
            pltpu.VMEM((8,) + half, BF16),
            pltpu.VMEM((8,) + half, BF16),
            pltpu.VMEM((4,) + half, BF16),
            pltpu.VMEM((4,) + half, BF16),
            pltpu.VMEM((4,) + half, BF16),
        ]
        + [pltpu.VMEM((ROUNDS,) + half, BF16)] * 8
        + [
            pltpu.SemaphoreType.DMA((COPIES,)),
            pltpu.SemaphoreType.DMA((COPIES,)),
            pltpu.SemaphoreType.DMA,
        ],
        compiler_params=pltpu.CompilerParams(collective_id=1, has_side_effects=True, vmem_limit_bytes=16 * MIB),
        name="exchange",
    )(pairings, subset, panel)


def whiten(raw_strain, fir_taps, block_slot):
    high, low, tc, ts = forward_tables()
    taps = jnp.pad(fir_taps, (0, 128 - TAPS)).reshape(1, 128)
    return pl.pallas_call(
        whiten_kernel,
        out_shape=jax.ShapeDtypeStruct((2, 2 * CH, HALF), BF16),
        in_specs=[pl.BlockSpec(memory_space=pltpu.VMEM)] * 7,
        out_specs=pl.BlockSpec(memory_space=pltpu.VMEM),
        scratch_shapes=[pltpu.VMEM((PIECES * CH, PIECE), BF16)] * 2 + [pltpu.VMEM((CH, NBIN), F32)] * 2,
        compiler_params=pltpu.CompilerParams(vmem_limit_bytes=48 * MIB),
    )(raw_strain, taps, block_slot.reshape(1, CH), high, low, tc, ts)


def correlate(own, theirs):
    cosine, sine, turn, flip = lag_tables()
    rows = OWN_STEP * CH
    steps = CH // OWN_STEP
    whole = lambda r, i: (0, 0)
    return pl.pallas_call(
        correlate_kernel,
        grid=(ROUNDS, steps),
        out_shape=jax.ShapeDtypeStruct((ROUNDS * CH * CH, 2 * LAG), BF16),
        in_specs=[
            pl.BlockSpec((2, 2 * CH, HALF), lambda r, i: (0, 0, 0)),
            pl.BlockSpec((1, 2, 2 * CH, HALF), lambda r, i: (r, 0, 0, 0)),
            pl.BlockSpec((NBIN, LAG), whole),
            pl.BlockSpec((NBIN, LAG), whole),
            pl.BlockSpec((2, NBIN), whole),
            pl.BlockSpec((256, 256), whole),
        ],
        out_specs=pl.BlockSpec((rows, 2 * LAG), lambda r, i: (r * steps + i, 0)),
        scratch_shapes=[pltpu.VMEM((2, CH, NBIN), F32)] + [pltpu.VMEM((rows, NBIN), BF16)] * 2,
        compiler_params=pltpu.CompilerParams(vmem_limit_bytes=48 * MIB),
    )(own, theirs, cosine, sine, turn, flip)


def per_device(raw_strain, fir_taps, block_slot, pairings, pair_subset):
    panel = whiten(raw_strain, fir_taps, block_slot)
    theirs = exchange(panel, pairings, pair_subset.reshape(ROUNDS, 1))
    result = correlate(panel, theirs)
    return result.reshape(ROUNDS, KSUB, CH, CH, 2 * LAG)


def solution(mesh):
    in_specs = (
        P(("group", "member"), None),
        P(),
        P(("group", "member")),
        P(None, "group"),
        P(None, "member", None),
    )
    out_specs = P(None, None, ("group", "member"), None, None)
    return jax.shard_map(
        per_device, mesh=mesh, in_specs=in_specs, out_specs=out_specs, check_vma=False
    )
```

```python
import functools
import math

import jax
import jax.numpy as jnp
import ml_dtypes
import numpy as np
from jax import lax
from jax.experimental import pallas as pl
from jax.experimental.pallas import tpu as pltpu
from jax.sharding import PartitionSpec as P

SEG = 2048
TAPS = 64
NFFT = 4096
F0 = 24
NBIN = 1024
WIN = 64
LAG = 1024
ROUNDS = 2
KSUB = 1
CH = 40
RAW = 4160
EPS = 1e-06

PIECE = 256
PIECES = SEG // PIECE
SPAN = 640
OWN_STEP = 8
MIB = 1 << 20
GRANT = 63 * MIB
BF16 = jnp.bfloat16
F32 = jnp.float32


def split_bf16(table):
    high = table.astype(ml_dtypes.bfloat16)
    low = (table - high.astype(np.float64)).astype(ml_dtypes.bfloat16)
    return high, low


def forward_tables():
    bins = F0 + np.arange(NBIN)
    phases = np.arange(PIECE)[:, None] * bins[None, :] % NFFT * (2.0 * math.pi / NFFT)
    high, low = split_bf16(np.concatenate([np.cos(phases), -np.sin(phases)], axis=1))
    shift = np.arange(PIECES)[:, None] * PIECE * bins[None, :] % NFFT * (2.0 * math.pi / NFFT)
    return np.stack([high, low]), np.stack([np.cos(shift), -np.sin(shift)]).astype(np.float32)


def lag_tables():
    bins = F0 + np.arange(NBIN)
    phases = bins[:, None] * (2 * np.arange(LAG) + 1)[None, :] % (2 * NFFT) * (math.pi / NFFT)
    scale = 1.0 / math.sqrt(NBIN)
    cosine = (np.cos(phases) * scale).astype(ml_dtypes.bfloat16)
    sine = (-np.sin(phases) * scale).astype(ml_dtypes.bfloat16)
    half = bins * (math.pi / NFFT)
    turn = np.stack([np.cos(half), -np.sin(half)]).astype(np.float32)
    return np.stack([cosine, sine]), turn


def dot(a, b):
    return jnp.dot(a, b, preferred_element_type=F32)


def parts(x):
    high = x.astype(BF16)
    return high, (x - high.astype(F32)).astype(BF16)


def whiten_block(raw_ref, taps_ref, slot_ref, tables_ref, shift_ref, panel_ref, filter_ref, dh_ref, dl_ref, re_ref, im_ref, loads):
    for load in loads[:3]:
        load.wait()
    filter_ref[...] = jnp.zeros((1, SPAN), F32)
    filter_ref[:, :TAPS] = taps_ref[...]
    filter_rows = pltpu.roll(jnp.broadcast_to(filter_ref[...], (PIECE, SPAN)), 0, 1, stride=2, stride_axis=0)
    pieces = [raw_ref[:, 2 * PIECE * b : 2 * PIECE * b + SPAN] for b in range(PIECES - 1)]
    last = raw_ref[:, 2 * PIECE * (PIECES - 1) :]
    pieces.append(jnp.concatenate([last, jnp.zeros((CH, SPAN - last.shape[1]), F32)], axis=1))
    xh, xl = parts(jnp.concatenate(pieces, axis=0))
    fh, fl = parts(filter_rows)
    contract = functools.partial(
        lax.dot_general, dimension_numbers=(((1,), (1,)), ((), ())), preferred_element_type=F32
    )
    dh, dl = parts(contract(xh, fh) + contract(xl, fh) + contract(xh, fl))
    dh_ref[...] = dh
    dl_ref[...] = dl
    for load in loads[3:]:
        load.wait()
    width = 256
    for n in range(NBIN // width):
        cols = slice(width * n, width * (n + 1))
        both = []
        for base in (0, NBIN):
            at = slice(base + width * n, base + width * (n + 1))
            wide = dh_ref[...]
            both.append(
                dot(wide, tables_ref[0, :, at]) + dot(dl_ref[...], tables_ref[0, :, at]) + dot(wide, tables_ref[1, :, at])
            )
        yr, yi = both
        re = jnp.zeros((CH, width), F32)
        im = jnp.zeros((CH, width), F32)
        for b in range(PIECES):
            tc = shift_ref[0, b : b + 1, cols]
            ts = shift_ref[1, b : b + 1, cols]
            r, i = yr[CH * b : CH * (b + 1)], yi[CH * b : CH * (b + 1)]
            re += r * tc - i * ts
            im += r * ts + i * tc
        re_ref[:, cols] = re
        im_ref[:, cols] = im
    re, im = re_ref[...], im_ref[...]
    total = re * re + im * im
    for step in (1, 2, 4, 8, 16, 32):
        total = total + pltpu.roll(total, NBIN - step, 1)
    total = pltpu.roll(total, WIN // 2, 1)
    col = lax.broadcasted_iota(jnp.int32, (CH, NBIN), 1)
    first, final = WIN // 2, NBIN - WIN // 2
    total = jnp.where(col < first, total[:, first : first + 1], total)
    total = jnp.where(col > final, total[:, final : final + 1], total)
    inverse = lax.rsqrt(total * (1.0 / WIN) + EPS)
    place = (lax.broadcasted_iota(jnp.int32, (CH, CH), 0) == slot_ref[...]).astype(F32).astype(BF16)
    re = dot(place, (re * inverse).astype(BF16))
    im = dot(place, (im * inverse).astype(BF16))
    for n in range(2):
        cols = slice(HALF * n, HALF * (n + 1))
        panel_ref[n] = jnp.concatenate([re[:, cols], im[:, cols]], axis=0).astype(BF16)


def whole_bins(panel):
    wide = panel.astype(F32)
    return (
        jnp.concatenate([wide[0, :CH], wide[1, :CH]], axis=1),
        jnp.concatenate([wide[0, CH:], wide[1, CH:]], axis=1),
    )


def correlate_kernel(own_ref, their_ref, lag_hbm, turn_ref, out_ref, lag_ref, turned_ref, cre_ref, cim_ref, load_sem):
    first = (pl.program_id(0) == 0) & (pl.program_id(1) == 0)
    loads = [pltpu.make_async_copy(lag_hbm.at[n], lag_ref.at[n], load_sem.at[n]) for n in range(2)]

    @pl.when(first)
    def _():
        for load in loads:
            load.start()
        own_re, own_im = whole_bins(own_ref[...])
        tr, ti = turn_ref[0:1, :], turn_ref[1:2, :]
        turned_ref[0] = own_re * tr - own_im * ti
        turned_ref[1] = own_re * ti + own_im * tr
        for load in loads:
            load.wait()

    br, bi = whole_bins(their_ref[0])
    at = pl.ds(pl.multiple_of(pl.program_id(1) * OWN_STEP, OWN_STEP), OWN_STEP)
    ar, ai = turned_ref[0, at, :], turned_ref[1, at, :]
    for i in range(0, OWN_STEP, 2):
        res, ims = [], []
        for k in (i, i + 1):
            r, m = ar[k : k + 1], ai[k : k + 1]
            res.append(r * br + m * bi)
            ims.append(m * br - r * bi)
        rows = slice(CH * i, CH * (i + 2))
        cre_ref[rows, :] = jnp.concatenate(res, axis=0).astype(BF16)
        cim_ref[rows, :] = jnp.concatenate(ims, axis=0).astype(BF16)
    backwards = 127 - lax.broadcasted_iota(jnp.int32, (OWN_STEP * CH, 128), 1)
    width = 512
    for n in range(LAG // width):
        cols = slice(width * n, width * (n + 1))
        even = dot(cre_ref[...], lag_ref[0, :, cols])
        odd = dot(cim_ref[...], lag_ref[1, :, cols])
        out_ref[:, LAG + width * n : LAG + width * (n + 1)] = (even + odd).astype(BF16)
        for q in range(width // 128):
            piece = even[:, 128 * q : 128 * (q + 1)] - odd[:, 128 * q : 128 * (q + 1)]
            piece = jnp.take_along_axis(piece, backwards, axis=1, mode="promise_in_bounds")
            low = LAG - width * n - 128 * (q + 1)
            out_ref[:, low : low + 128] = piece.astype(BF16)


HALF = NBIN // 2
MESH_ID = pl.DeviceIdType.MESH


def choose(first, a, b):
    return jnp.where(first, a.astype(F32), b.astype(F32)).astype(BF16)


def exchange_kernel(pairings_ref, subset_ref, raw_hbm, taps_hbm, slot_hbm, tables_hbm, shift_hbm, panel_ref, theirs_ref,
                    raw_ref, taps_ref, slot_ref, tables_ref, shift_ref, filter_ref, dh_ref, dl_ref, re_ref, im_ref, load_sem,
                    meta, peers, flat, row, rows0, rows1, line, lines0, lines1,
                    row_in, rows_in, line_in, lines_in, row_out, rows_out, line_out, lines_out, send, recv, local):
    g, m = lax.axis_index("group"), lax.axis_index("member")
    z, h = g // 2, g % 2
    l, x, c = m // 8, (m // 2) % 4, m % 2
    k = x * 2 + c

    def at(dz=0, dh=0, dl=0, dx=0, dc=0):
        group = lax.rem(z + dz, 4) * 2 + lax.rem(h + dh, 2)
        member = lax.rem(l + dl, 2) * 8 + lax.rem(x + dx, 4) * 2 + lax.rem(c + dc, 2)
        return group, member

    along_x = [at(dx=d) for d in (1, 3, 2)]
    along_z = [at(dz=d) for d in (1, 3, 2)]
    core, low, high = at(dc=1), at(dl=1), at(dh=1)
    started = []

    def put(src, dst, where):
        n = len(started)
        copy = pltpu.make_async_remote_copy(
            src_ref=src, dst_ref=dst, send_sem=send.at[n], recv_sem=recv.at[n], device_id=where, device_id_type=MESH_ID
        )
        copy.start()
        started.append(copy)
        return copy

    barrier = pltpu.get_barrier_semaphore()
    everyone = along_x + along_z + [core, low, high]
    for where in everyone:
        pl.semaphore_signal(barrier, inc=1, device_id=where, device_id_type=MESH_ID)

    loads = []
    moves = ((raw_hbm, raw_ref), (taps_hbm, taps_ref), (slot_hbm, slot_ref), (tables_hbm, tables_ref), (shift_hbm, shift_ref))
    for n, (src, dst) in enumerate(moves):
        loads.append(pltpu.make_async_copy(src, dst, load_sem.at[n]))
        loads[-1].start()
    index = lax.broadcasted_iota(jnp.int32, (8, 128), 0)
    mine = jnp.zeros((8, 128), jnp.int32)
    for r in range(ROUNDS):
        mine = jnp.where(index == r, pairings_ref[r], mine)
        mine = jnp.where(index == ROUNDS + r, subset_ref[r], mine)
    meta[...] = mine
    whiten_block(
        raw_ref, taps_ref, slot_ref, tables_ref, shift_ref, panel_ref, filter_ref, dh_ref, dl_ref, re_ref, im_ref, loads
    )
    pl.semaphore_wait(barrier, len(everyone))

    asks = [put(meta, peers.at[0], low), put(meta, peers.at[1], high)]
    row[k] = panel_ref[0]
    line[z] = panel_ref[1]
    row_x = [put(panel_ref.at[0], row.at[k], where) for where in along_x]
    line_z = [put(panel_ref.at[1], line.at[z], where) for where in along_z]
    row_c = [put(panel_ref.at[0], row.at[k], core)]
    for ask in asks:
        ask.wait_recv()
    fetch = pltpu.make_async_copy(peers, flat, local)
    fetch.start()
    fetch.wait()
    my_pair = [pairings_ref[r] for r in range(ROUNDS)]
    my_sub = [subset_ref[r] for r in range(ROUNDS)]
    low_sub = [flat[0, ROUNDS + r, 0] for r in range(ROUNDS)]
    high_pair = [flat[1, r, 0] for r in range(ROUNDS)]

    def slot(dx):
        return lax.rem(x + dx, 4) * 2 + c

    for copy, dx in zip(row_x, (3, 1, 2)):
        copy.wait_recv()
        row_c.append(put(row.at[slot(dx)], row.at[slot(dx)], core))
    for copy in line_z:
        copy.wait_recv()
    rows, lines = (rows0, rows1), (lines0, lines1)
    in_group = [lax.rem(my_pair[r], 2) == h for r in range(ROUNDS)]
    in_member = [my_sub[r] // 8 == l for r in range(ROUNDS)]
    my_z = [my_pair[r] // 2 for r in range(ROUNDS)]
    my_k = [lax.rem(my_sub[r], 8) for r in range(ROUNDS)]
    line_y = []
    for r in range(ROUNDS):
        line_out[r] = line[high_pair[r] // 2]
        line_y.append(put(line_out.at[r], line_in.at[r], high))
    for copy in row_c:
        copy.wait_recv()
    row_y = []
    for r in range(ROUNDS):
        row_out[r] = row[lax.rem(low_sub[r], 8)]
        row_y.append(put(row_out.at[r], row_in.at[r], low))

    rows_x, rows_c, lines_z = [], [], []
    for r in range(ROUNDS):
        line_y[r].wait_recv()
        rows[r][k] = choose(in_group[r], line[my_z[r]], line_in[r])
        own = rows[r].at[k]
        rows_x.append([put(own, own, where) for where in along_x])
        rows_c.append([put(own, own, core)])
        row_y[r].wait_recv()
        lines[r][z] = choose(in_member[r], row[my_k[r]], row_in[r])
        own = lines[r].at[z]
        lines_z.append([put(own, own, where) for where in along_z])
    last_line, last_row = [], []
    for r in range(ROUNDS):
        for copy, dx in zip(rows_x[r], (3, 1, 2)):
            copy.wait_recv()
            got = rows[r].at[slot(dx)]
            rows_c[r].append(put(got, got, core))
        for copy in lines_z[r]:
            copy.wait_recv()
        lines_out[r] = lines[r][high_pair[r] // 2]
        last_line.append(put(lines_out.at[r], lines_in.at[r], high))
        for copy in rows_c[r]:
            copy.wait_recv()
        rows_out[r] = rows[r][lax.rem(low_sub[r], 8)]
        last_row.append(put(rows_out.at[r], rows_in.at[r], low))
    for r in range(ROUNDS):
        last_line[r].wait_recv()
        theirs_ref[r, 0] = choose(in_group[r], lines[r][my_z[r]], lines_in[r])
        last_row[r].wait_recv()
        theirs_ref[r, 1] = choose(in_member[r], rows[r][my_k[r]], rows_in[r])
    for copy in started:
        copy.wait_send()


COPIES = 2 + 7 + 3 + 2 + 2 + 14 + 6 + 2 + 2


def exchange(raw_strain, fir_taps, block_slot, pairings, subset):
    half = (2 * CH, HALF)
    tables, shift = forward_tables()
    return pl.pallas_call(
        exchange_kernel,
        out_shape=(
            jax.ShapeDtypeStruct((2,) + half, BF16),
            jax.ShapeDtypeStruct((ROUNDS, 2) + half, BF16),
        ),
        in_specs=[pl.BlockSpec(memory_space=pltpu.SMEM)] * 2 + [pl.BlockSpec(memory_space=pltpu.HBM)] * 5,
        out_specs=(pl.BlockSpec(memory_space=pltpu.VMEM), pl.BlockSpec(memory_space=pltpu.VMEM)),
        scratch_shapes=[
            pltpu.VMEM((CH, RAW), F32),
            pltpu.VMEM((1, TAPS), F32),
            pltpu.VMEM((1, CH), jnp.int32),
            pltpu.VMEM((2, PIECE, 2 * NBIN), BF16),
            pltpu.VMEM((2, PIECES, NBIN), F32),
            pltpu.VMEM((1, SPAN), F32),
            pltpu.VMEM((PIECES * CH, PIECE), BF16),
            pltpu.VMEM((PIECES * CH, PIECE), BF16),
            pltpu.VMEM((CH, NBIN), F32),
            pltpu.VMEM((CH, NBIN), F32),
            pltpu.SemaphoreType.DMA((5,)),
            pltpu.VMEM((8, 128), jnp.int32),
            pltpu.VMEM((2, 8, 128), jnp.int32),
            pltpu.SMEM((2, 8, 128), jnp.int32),
            pltpu.VMEM((8,) + half, BF16),
            pltpu.VMEM((8,) + half, BF16),
            pltpu.VMEM((8,) + half, BF16),
            pltpu.VMEM((4,) + half, BF16),
            pltpu.VMEM((4,) + half, BF16),
            pltpu.VMEM((4,) + half, BF16),
        ]
        + [pltpu.VMEM((ROUNDS,) + half, BF16)] * 8
        + [
            pltpu.SemaphoreType.DMA((COPIES,)),
            pltpu.SemaphoreType.DMA((COPIES,)),
            pltpu.SemaphoreType.DMA,
        ],
        compiler_params=pltpu.CompilerParams(collective_id=1, has_side_effects=True, vmem_limit_bytes=GRANT),
        name="exchange",
    )(pairings, subset, raw_strain, fir_taps.reshape(1, TAPS), block_slot.reshape(1, CH), tables, shift)


def correlate(own, theirs):
    lags, turn = lag_tables()
    rows = OWN_STEP * CH
    steps = CH // OWN_STEP
    whole = lambda r, i: (0, 0)
    return pl.pallas_call(
        correlate_kernel,
        grid=(ROUNDS, steps),
        out_shape=jax.ShapeDtypeStruct((ROUNDS * CH * CH, 2 * LAG), BF16),
        in_specs=[
            pl.BlockSpec((2, 2 * CH, HALF), lambda r, i: (0, 0, 0)),
            pl.BlockSpec((1, 2, 2 * CH, HALF), lambda r, i: (r, 0, 0, 0)),
            pl.BlockSpec(memory_space=pltpu.HBM),
            pl.BlockSpec((2, NBIN), whole),
        ],
        out_specs=pl.BlockSpec((rows, 2 * LAG), lambda r, i: (r * steps + i, 0)),
        scratch_shapes=[
            pltpu.VMEM((2, NBIN, LAG), BF16),
            pltpu.VMEM((2, CH, NBIN), F32),
            pltpu.VMEM((rows, NBIN), BF16),
            pltpu.VMEM((rows, NBIN), BF16),
            pltpu.SemaphoreType.DMA((2,)),
        ],
        compiler_params=pltpu.CompilerParams(vmem_limit_bytes=GRANT),
    )(own, theirs, lags, turn)


def per_device(raw_strain, fir_taps, block_slot, pairings, pair_subset):
    panel, theirs = exchange(
        raw_strain, fir_taps, block_slot, pairings.reshape(ROUNDS), pair_subset.reshape(ROUNDS)
    )
    result = correlate(panel, theirs)
    return result.reshape(ROUNDS, KSUB, CH, CH, 2 * LAG)


def solution(mesh):
    in_specs = (
        P(("group", "member"), None),
        P(),
        P(("group", "member")),
        P(None, "group"),
        P(None, "member", None),
    )
    out_specs = P(None, None, ("group", "member"), None, None)
    return jax.shard_map(
        per_device, mesh=mesh, in_specs=in_specs, out_specs=out_specs, check_vma=False
    )
```

```python
import functools
import math

import jax
import jax.numpy as jnp
import ml_dtypes
import numpy as np
from jax import lax
from jax.experimental import pallas as pl
from jax.experimental.pallas import tpu as pltpu
from jax.sharding import PartitionSpec as P

SEG = 2048
TAPS = 64
NFFT = 4096
F0 = 24
NBIN = 1024
WIN = 64
LAG = 1024
ROUNDS = 2
KSUB = 1
CH = 40
RAW = 4160
EPS = 1e-06

PIECE = 256
PIECES = SEG // PIECE
SPAN = 640
OWN_STEP = 8
MIB = 1 << 20
CLASSES = (0, 2, 1, 3)
QUARTER = NBIN // 4
GRANT = 63 * MIB
CHUNKS = 4
BINS = NBIN // CHUNKS
BF16 = jnp.bfloat16
F32 = jnp.float32


def split_bf16(table):
    high = table.astype(ml_dtypes.bfloat16)
    low = (table - high.astype(np.float64)).astype(ml_dtypes.bfloat16)
    return high, low


def bin_order():
    return np.concatenate([np.arange(r, NBIN, 4) for r in CLASSES])


def forward_tables():
    bins = F0 + bin_order()
    phases = np.arange(PIECE)[:, None] * bins[None, :] % NFFT * (2.0 * math.pi / NFFT)
    high, low = split_bf16(np.concatenate([np.cos(phases), -np.sin(phases)], axis=1))
    shift = np.arange(PIECES)[:, None] * PIECE * bins[None, :] % NFFT * (2.0 * math.pi / NFFT)
    return np.stack([high, low]), np.stack([np.cos(shift), -np.sin(shift)]).astype(np.float32)


def lag_tables():
    bins = F0 + bin_order()
    phases = bins[:, None] * (2 * np.arange(LAG) + 1)[None, :] % (2 * NFFT) * (math.pi / NFFT)
    scale = 1.0 / math.sqrt(NBIN)
    cosine = (np.cos(phases) * scale).astype(ml_dtypes.bfloat16)
    sine = (-np.sin(phases) * scale).astype(ml_dtypes.bfloat16)
    half = bins * (math.pi / NFFT)
    turn = np.stack([np.cos(half), -np.sin(half)]).astype(np.float32)
    return np.stack([cosine, sine]), turn


def dot(a, b):
    return jnp.dot(a, b, preferred_element_type=F32)


def parts(x):
    high = x.astype(BF16)
    return high, (x - high.astype(F32)).astype(BF16)


def whiten_block(raw_ref, taps_ref, slot_ref, tables_ref, shift_ref, panel_ref, filter_ref, dh_ref, dl_ref, re_ref, im_ref, loads):
    for load in loads[:3]:
        load.wait()
    filter_ref[...] = jnp.zeros((1, SPAN), F32)
    filter_ref[:, :TAPS] = taps_ref[...]
    filter_rows = pltpu.roll(jnp.broadcast_to(filter_ref[...], (PIECE, SPAN)), 0, 1, stride=2, stride_axis=0)
    pieces = [raw_ref[:, 2 * PIECE * b : 2 * PIECE * b + SPAN] for b in range(PIECES - 1)]
    last = raw_ref[:, 2 * PIECE * (PIECES - 1) :]
    pieces.append(jnp.concatenate([last, jnp.zeros((CH, SPAN - last.shape[1]), F32)], axis=1))
    xh, xl = parts(jnp.concatenate(pieces, axis=0))
    fh, fl = parts(filter_rows)
    contract = functools.partial(
        lax.dot_general, dimension_numbers=(((1,), (1,)), ((), ())), preferred_element_type=F32
    )
    dh, dl = parts(contract(xh, fh) + contract(xl, fh) + contract(xh, fl))
    dh_ref[...] = dh
    dl_ref[...] = dl
    for load in loads[3:]:
        load.wait()
    width = 256
    for n in range(NBIN // width):
        cols = slice(width * n, width * (n + 1))
        both = []
        for base in (0, NBIN):
            at = slice(base + width * n, base + width * (n + 1))
            wide = dh_ref[...]
            both.append(
                dot(wide, tables_ref[0, :, at]) + dot(dl_ref[...], tables_ref[0, :, at]) + dot(wide, tables_ref[1, :, at])
            )
        yr, yi = both
        re = jnp.zeros((CH, width), F32)
        im = jnp.zeros((CH, width), F32)
        for b in range(PIECES):
            tc = shift_ref[0, b : b + 1, cols]
            ts = shift_ref[1, b : b + 1, cols]
            r, i = yr[CH * b : CH * (b + 1)], yi[CH * b : CH * (b + 1)]
            re += r * tc - i * ts
            im += r * ts + i * tc
        re_ref[:, cols] = re
        im_ref[:, cols] = im
    re, im = re_ref[...], im_ref[...]
    power = re * re + im * im
    sums = {}
    for place_of, r in enumerate(CLASSES):
        total = power[:, QUARTER * place_of : QUARTER * (place_of + 1)]
        for step in (1, 2, 4, 8):
            total = total + pltpu.roll(total, QUARTER - step, 1)
        sums[r] = total
    later = {r: pltpu.roll(sums[r], QUARTER - 1, 1) for r in range(3)}
    col = lax.broadcasted_iota(jnp.int32, (CH, QUARTER), 1)
    edge = WIN // 8
    whole = sums[0] + sums[1] + sums[2] + sums[3]
    first, final = whole[:, :1], whole[:, QUARTER - 2 * edge : QUARTER - 2 * edge + 1]
    bands = []
    for r in CLASSES:
        total = sum(later[n] if n < r else sums[n] for n in range(4))
        total = pltpu.roll(total, edge, 1)
        total = jnp.where(col < edge, first, total)
        bands.append(jnp.where(col >= QUARTER - edge, final, total))
    inverse = lax.rsqrt(jnp.concatenate(bands, axis=1) * (1.0 / WIN) + EPS)
    place = (lax.broadcasted_iota(jnp.int32, (CH, CH), 0) == slot_ref[...]).astype(F32).astype(BF16)
    re = dot(place, (re * inverse).astype(BF16))
    im = dot(place, (im * inverse).astype(BF16))
    for n in range(CHUNKS):
        cols = slice(BINS * n, BINS * (n + 1))
        panel_ref[n] = jnp.concatenate([re[:, cols], im[:, cols]], axis=0).astype(BF16)


def whole_bins(panel):
    wide = panel.astype(F32)
    return (
        jnp.concatenate([wide[n, :CH] for n in range(CHUNKS)], axis=1),
        jnp.concatenate([wide[n, CH:] for n in range(CHUNKS)], axis=1),
    )


def correlate_kernel(own_ref, their_ref, lag_hbm, turn_ref, out_ref, lag_ref, turned_ref, cre_ref, cim_ref, load_sem):
    first = (pl.program_id(0) == 0) & (pl.program_id(1) == 0)
    loads = [pltpu.make_async_copy(lag_hbm.at[n], lag_ref.at[n], load_sem.at[n]) for n in range(2)]

    @pl.when(first)
    def _():
        for load in loads:
            load.start()
        own_re, own_im = whole_bins(own_ref[...])
        tr, ti = turn_ref[0:1, :], turn_ref[1:2, :]
        turned_ref[0] = own_re * tr - own_im * ti
        turned_ref[1] = own_re * ti + own_im * tr
        for load in loads:
            load.wait()

    br, bi = whole_bins(their_ref[0])
    at = pl.ds(pl.multiple_of(pl.program_id(1) * OWN_STEP, OWN_STEP), OWN_STEP)
    ar, ai = turned_ref[0, at, :], turned_ref[1, at, :]
    for i in range(0, OWN_STEP, 2):
        res, ims = [], []
        for k in (i, i + 1):
            r, m = ar[k : k + 1], ai[k : k + 1]
            res.append(r * br + m * bi)
            ims.append(m * br - r * bi)
        rows = slice(CH * i, CH * (i + 2))
        cre_ref[rows, :] = jnp.concatenate(res, axis=0).astype(BF16)
        cim_ref[rows, :] = jnp.concatenate(ims, axis=0).astype(BF16)
    lag_rows(cre_ref, cim_ref, lag_ref, out_ref)


def lag_rows(cre_ref, cim_ref, lag_ref, out_ref):
    quarters = slice(0, QUARTER), slice(QUARTER, 2 * QUARTER), slice(2 * QUARTER, NBIN)
    backwards = 127 - lax.broadcasted_iota(jnp.int32, (OWN_STEP * CH, 128), 1)

    def mirror(value, low):
        for n in range(width // 128):
            piece = jnp.take_along_axis(value[:, 128 * n : 128 * (n + 1)], backwards, axis=1, mode="promise_in_bounds")
            yield slice(low + width - 128 * (n + 1), low + width - 128 * n), piece

    width = 256
    half = LAG // 2
    for n in range(half // width):
        near = slice(width * n, width * (n + 1))
        far = slice(LAG - width * (n + 1), LAG - width * n)
        even = [dot(cre_ref[:, rows], lag_ref[0, rows, near]) for rows in quarters[:2]]
        odd = [dot(cim_ref[:, rows], lag_ref[1, rows, near]) for rows in quarters[:2]]
        even_near = even[0] + even[1] + dot(cre_ref[:, quarters[2]], lag_ref[0, quarters[2], near])
        odd_near = odd[0] + odd[1] + dot(cim_ref[:, quarters[2]], lag_ref[1, quarters[2], near])
        out_ref[:, LAG + width * n : LAG + width * (n + 1)] = (even_near + odd_near).astype(BF16)
        for cols, piece in mirror(even_near - odd_near, LAG - width * (n + 1)):
            out_ref[:, cols] = piece.astype(BF16)
        even_far, odd_far = even[0] - even[1], odd[1] - odd[0]
        even_rest = dot(cre_ref[:, quarters[2]], lag_ref[0, quarters[2], far])
        odd_rest = dot(cim_ref[:, quarters[2]], lag_ref[1, quarters[2], far])
        rest = even_rest + odd_rest
        for cols, piece in mirror(even_far + odd_far, 0):
            out_ref[:, 2 * LAG - width * (n + 1) + cols.start : 2 * LAG - width * (n + 1) + cols.stop] = (piece + rest[:, cols]).astype(BF16)
        straight = even_far - odd_far
        for cols, piece in mirror(even_rest - odd_rest, 0):
            out_ref[:, width * n + cols.start : width * n + cols.stop] = (piece + straight[:, cols]).astype(BF16)


MESH_ID = pl.DeviceIdType.MESH


def choose(first, a, b):
    return jnp.where(first, a.astype(F32), b.astype(F32)).astype(BF16)


def exchange_kernel(pairings_ref, subset_ref, raw_hbm, taps_hbm, slot_hbm, tables_hbm, shift_hbm, panel_ref, theirs_ref,
                    raw_ref, taps_ref, slot_ref, tables_ref, shift_ref, filter_ref, dh_ref, dl_ref, re_ref, im_ref, load_sem,
                    meta, peers, flat, pair, *rest):
    shared, single = rest[:CHUNKS], rest[CHUNKS : CHUNKS * (1 + ROUNDS)]
    send, recv, local = rest[CHUNKS * (1 + ROUNDS) :]
    g, m = lax.axis_index("group"), lax.axis_index("member")
    z, h = g // 2, g % 2
    l, x, c = m // 8, (m // 2) % 4, m % 2
    k = x * 2 + c

    def at(dz=0, dh=0, dl=0, dx=0, dc=0):
        group = lax.rem(z + dz, 4) * 2 + lax.rem(h + dh, 2)
        member = lax.rem(l + dl, 2) * 8 + lax.rem(x + dx, 4) * 2 + lax.rem(c + dc, 2)
        return group, member

    along_x = [at(dx=d) for d in (1, 3, 2)]
    along_z = [at(dz=d) for d in (1, 3, 2)]
    core, low, high = at(dc=1), at(dl=1), at(dh=1)
    started = []

    def put(src, dst, where):
        n = len(started)
        copy = pltpu.make_async_remote_copy(
            src_ref=src, dst_ref=dst, send_sem=send.at[n], recv_sem=recv.at[n], device_id=where, device_id_type=MESH_ID
        )
        copy.start()
        started.append(copy)
        return copy

    barrier = pltpu.get_barrier_semaphore()
    everyone = along_x + along_z + [core, low, high]
    for where in everyone:
        pl.semaphore_signal(barrier, inc=1, device_id=where, device_id_type=MESH_ID)

    loads = []
    moves = ((raw_hbm, raw_ref), (taps_hbm, taps_ref), (slot_hbm, slot_ref), (tables_hbm, tables_ref), (shift_hbm, shift_ref))
    for n, (src, dst) in enumerate(moves):
        loads.append(pltpu.make_async_copy(src, dst, load_sem.at[n]))
        loads[-1].start()
    index = lax.broadcasted_iota(jnp.int32, (8, 128), 0)
    mine = jnp.zeros((8, 128), jnp.int32)
    for r in range(ROUNDS):
        mine = jnp.where(index == r, pairings_ref[r], mine)
        mine = jnp.where(index == ROUNDS + r, subset_ref[r], mine)
    meta[...] = mine
    whiten_block(
        raw_ref, taps_ref, slot_ref, tables_ref, shift_ref, panel_ref, filter_ref, dh_ref, dl_ref, re_ref, im_ref, loads
    )
    pl.semaphore_wait(barrier, len(everyone))

    asks = [put(meta, peers.at[0], low), put(meta, peers.at[1], high)]
    my_pair = [pairings_ref[r] for r in range(ROUNDS)]
    my_sub = [subset_ref[r] for r in range(ROUNDS)]
    in_group = [lax.rem(my_pair[r], 2) == h for r in range(ROUNDS)]
    in_member = [my_sub[r] // 8 == l for r in range(ROUNDS)]
    my_z = [my_pair[r] // 2 for r in range(ROUNDS)]
    my_k = [lax.rem(my_sub[r], 8) for r in range(ROUNDS)]
    even, odd = tuple(range(0, CHUNKS, 2)), tuple(range(1, CHUNKS, 2))
    hers = {}
    moving = {}

    def read_asks():
        for ask in asks:
            ask.wait_recv()
        fetch = pltpu.make_async_copy(peers, flat, local)
        fetch.start()
        fetch.wait()
        for r in range(ROUNDS):
            hers["k", r] = lax.rem(flat[0, ROUNDS + r, 0], 8)
            hers["z", r] = flat[1, r, 0] // 2

    def store(q, r):
        return shared[q] if r < 0 else single[q * ROUNDS + r]

    def by_row(q, r):
        return (q % 2 == 0) == (r < 0)

    def slot(dx):
        return lax.rem(x + dx, 4) * 2 + c

    def gather(q, r):
        room = store(q, r)
        if by_row(q, r):
            own, targets = room.at[k], along_x + [core]
        else:
            own, targets = room.at[z], along_z
        src = own
        if r < 0:
            room[k if by_row(q, r) else z] = panel_ref[q]
            src = panel_ref.at[q]
        moving[q, r] = [put(src, own, where) for where in targets]

    def forward(q, r):
        if by_row(q, r):
            room, copies = store(q, r), moving[q, r]
            for copy, dx in zip(copies[:3], (3, 1, 2)):
                copy.wait_recv()
                got = room.at[slot(dx)]
                copies.append(put(got, got, core))
            del copies[:3]

    def ask_pair(q, stage, r):
        if (q, stage) in moving:
            for copy in moving.pop((q, stage)):
                copy.wait_recv()
        out, into = (0, 1) if stage < 0 else (2, 3)
        row = by_row(q, stage)
        pair[q, r, out] = store(q, stage)[hers["k" if row else "z", r]]
        moving[q, stage, r] = put(pair.at[q, r, out], pair.at[q, r, into], low if row else high)

    def chosen(q, stage, r):
        moving.pop((q, stage, r)).wait_recv()
        into = pair[q, r, 1 if stage < 0 else 3]
        if by_row(q, stage):
            return choose(in_member[r], store(q, stage)[my_k[r]], into)
        return choose(in_group[r], store(q, stage)[my_z[r]], into)

    def regroup(q, r):
        single[q * ROUNDS + r][k if by_row(q, r) else z] = chosen(q, -1, r)
        gather(q, r)

    def finish(q, r):
        theirs_ref[r, q] = chosen(q, r, r)

    for q in range(CHUNKS):
        gather(q, -1)
    read_asks()
    for q in even:
        forward(q, -1)
    for r in range(ROUNDS):
        for q in odd + even:
            ask_pair(q, -1, r)
    for r in range(ROUNDS):
        for q in odd + even:
            regroup(q, r)
    for r in range(ROUNDS):
        for q in odd:
            forward(q, r)
        for q in even + odd:
            ask_pair(q, r, r)
    for r in range(ROUNDS):
        for q in even + odd:
            finish(q, r)
    for copy in started:
        copy.wait_send()


COPIES = 2 + CHUNKS // 2 * 38


def exchange(raw_strain, fir_taps, block_slot, pairings, subset):
    part = (2 * CH, BINS)
    tables, shift = forward_tables()
    return pl.pallas_call(
        exchange_kernel,
        out_shape=(
            jax.ShapeDtypeStruct((CHUNKS,) + part, BF16),
            jax.ShapeDtypeStruct((ROUNDS, CHUNKS) + part, BF16),
        ),
        in_specs=[pl.BlockSpec(memory_space=pltpu.SMEM)] * 2 + [pl.BlockSpec(memory_space=pltpu.HBM)] * 5,
        out_specs=(pl.BlockSpec(memory_space=pltpu.VMEM), pl.BlockSpec(memory_space=pltpu.VMEM)),
        scratch_shapes=[
            pltpu.VMEM((CH, RAW), F32),
            pltpu.VMEM((1, TAPS), F32),
            pltpu.VMEM((1, CH), jnp.int32),
            pltpu.VMEM((2, PIECE, 2 * NBIN), BF16),
            pltpu.VMEM((2, PIECES, NBIN), F32),
            pltpu.VMEM((1, SPAN), F32),
            pltpu.VMEM((PIECES * CH, PIECE), BF16),
            pltpu.VMEM((PIECES * CH, PIECE), BF16),
            pltpu.VMEM((CH, NBIN), F32),
            pltpu.VMEM((CH, NBIN), F32),
            pltpu.SemaphoreType.DMA((5,)),
            pltpu.VMEM((8, 128), jnp.int32),
            pltpu.VMEM((2, 8, 128), jnp.int32),
            pltpu.SMEM((2, 8, 128), jnp.int32),
            pltpu.VMEM((CHUNKS, ROUNDS, 4) + part, BF16),
        ]
        + [pltpu.VMEM((8 if q % 2 == 0 else 4,) + part, BF16) for q in range(CHUNKS)]
        + [pltpu.VMEM((4 if q % 2 == 0 else 8,) + part, BF16) for q in range(CHUNKS) for r in range(ROUNDS)]
        + [
            pltpu.SemaphoreType.DMA((COPIES,)),
            pltpu.SemaphoreType.DMA((COPIES,)),
            pltpu.SemaphoreType.DMA,
        ],
        compiler_params=pltpu.CompilerParams(collective_id=1, has_side_effects=True, vmem_limit_bytes=GRANT),
        name="exchange",
    )(pairings, subset, raw_strain, fir_taps.reshape(1, TAPS), block_slot.reshape(1, CH), tables, shift)


def correlate(own, theirs):
    lags, turn = lag_tables()
    rows = OWN_STEP * CH
    steps = CH // OWN_STEP
    whole = lambda r, i: (0, 0)
    return pl.pallas_call(
        correlate_kernel,
        grid=(ROUNDS, steps),
        out_shape=jax.ShapeDtypeStruct((ROUNDS * CH * CH, 2 * LAG), BF16),
        in_specs=[
            pl.BlockSpec((CHUNKS, 2 * CH, BINS), lambda r, i: (0, 0, 0)),
            pl.BlockSpec((1, CHUNKS, 2 * CH, BINS), lambda r, i: (r, 0, 0, 0)),
            pl.BlockSpec(memory_space=pltpu.HBM),
            pl.BlockSpec((2, NBIN), whole),
        ],
        out_specs=pl.BlockSpec((rows, 2 * LAG), lambda r, i: (r * steps + i, 0)),
        scratch_shapes=[
            pltpu.VMEM((2, NBIN, LAG), BF16),
            pltpu.VMEM((2, CH, NBIN), F32),
            pltpu.VMEM((rows, NBIN), BF16),
            pltpu.VMEM((rows, NBIN), BF16),
            pltpu.SemaphoreType.DMA((2,)),
        ],
        compiler_params=pltpu.CompilerParams(vmem_limit_bytes=GRANT),
    )(own, theirs, lags, turn)


def per_device(raw_strain, fir_taps, block_slot, pairings, pair_subset):
    panel, theirs = exchange(
        raw_strain, fir_taps, block_slot, pairings.reshape(ROUNDS), pair_subset.reshape(ROUNDS)
    )
    result = correlate(panel, theirs)
    return result.reshape(ROUNDS, KSUB, CH, CH, 2 * LAG)


def solution(mesh):
    in_specs = (
        P(("group", "member"), None),
        P(),
        P(("group", "member")),
        P(None, "group"),
        P(None, "member", None),
    )
    out_specs = P(None, None, ("group", "member"), None, None)
    return jax.shard_map(
        per_device, mesh=mesh, in_specs=in_specs, out_specs=out_specs, check_vma=False
    )
```

```python
import functools
import math

import jax
import jax.numpy as jnp
import ml_dtypes
import numpy as np
from jax import lax
from jax.experimental import pallas as pl
from jax.experimental.pallas import tpu as pltpu
from jax.sharding import PartitionSpec as P

SEG = 2048
TAPS = 64
NFFT = 4096
F0 = 24
NBIN = 1024
WIN = 64
LAG = 1024
ROUNDS = 2
KSUB = 1
CH = 40
RAW = 4160
EPS = 1e-06

PIECE = 256
PIECES = SEG // PIECE
SPAN = 640
OWN_STEP = 8
MIB = 1 << 20
CLASSES = (0, 2, 1, 3)
QUARTER = NBIN // 4
GRANT = 63 * MIB
CHUNKS = 4
BINS = NBIN // CHUNKS
BF16 = jnp.bfloat16
F32 = jnp.float32


def split_bf16(table):
    high = table.astype(ml_dtypes.bfloat16)
    low = (table - high.astype(np.float64)).astype(ml_dtypes.bfloat16)
    return high, low


def bin_order():
    return np.concatenate([np.arange(r, NBIN, 4) for r in CLASSES])


def forward_tables():
    bins = F0 + bin_order()
    phases = np.arange(PIECE)[:, None] * bins[None, :] % NFFT * (2.0 * math.pi / NFFT)
    high, low = split_bf16(np.concatenate([np.cos(phases), -np.sin(phases)], axis=1))
    shift = np.arange(PIECES)[:, None] * PIECE * bins[None, :] % NFFT * (2.0 * math.pi / NFFT)
    return np.stack([high, low]), np.stack([np.cos(shift), -np.sin(shift)]).astype(np.float32)


def lag_tables():
    bins = F0 + bin_order()
    phases = bins[:, None] * (2 * np.arange(LAG) + 1)[None, :] % (2 * NFFT) * (math.pi / NFFT)
    scale = 1.0 / math.sqrt(NBIN)
    cosine = (np.cos(phases) * scale).astype(ml_dtypes.bfloat16)
    sine = (-np.sin(phases) * scale).astype(ml_dtypes.bfloat16)
    half = bins * (math.pi / NFFT)
    turn = np.stack([np.cos(half), -np.sin(half)]).astype(np.float32)
    return np.stack([cosine, sine]), turn


def dot(a, b):
    return jnp.dot(a, b, preferred_element_type=F32)


def parts(x):
    high = x.astype(BF16)
    return high, (x - high.astype(F32)).astype(BF16)


def whiten_block(raw_ref, taps_ref, slot_ref, tables_ref, shift_ref, panel_ref, filter_ref, dh_ref, dl_ref, re_ref, im_ref, loads):
    for load in loads[:3]:
        load.wait()
    filter_ref[...] = jnp.zeros((1, SPAN), F32)
    filter_ref[:, :TAPS] = taps_ref[...]
    filter_rows = pltpu.roll(jnp.broadcast_to(filter_ref[...], (PIECE, SPAN)), 0, 1, stride=2, stride_axis=0)
    pieces = [raw_ref[:, 2 * PIECE * b : 2 * PIECE * b + SPAN] for b in range(PIECES - 1)]
    last = raw_ref[:, 2 * PIECE * (PIECES - 1) :]
    pieces.append(jnp.concatenate([last, jnp.zeros((CH, SPAN - last.shape[1]), F32)], axis=1))
    xh, xl = parts(jnp.concatenate(pieces, axis=0))
    fh, fl = parts(filter_rows)
    contract = functools.partial(
        lax.dot_general, dimension_numbers=(((1,), (1,)), ((), ())), preferred_element_type=F32
    )
    dh, dl = parts(contract(xh, fh) + contract(xl, fh) + contract(xh, fl))
    dh_ref[...] = dh
    dl_ref[...] = dl
    for load in loads[3:]:
        load.wait()
    width = 256
    for n in range(NBIN // width):
        cols = slice(width * n, width * (n + 1))
        both = []
        for base in (0, NBIN):
            at = slice(base + width * n, base + width * (n + 1))
            wide = dh_ref[...]
            both.append(
                dot(wide, tables_ref[0, :, at]) + dot(dl_ref[...], tables_ref[0, :, at]) + dot(wide, tables_ref[1, :, at])
            )
        yr, yi = both
        re = jnp.zeros((CH, width), F32)
        im = jnp.zeros((CH, width), F32)
        for b in range(PIECES):
            tc = shift_ref[0, b : b + 1, cols]
            ts = shift_ref[1, b : b + 1, cols]
            r, i = yr[CH * b : CH * (b + 1)], yi[CH * b : CH * (b + 1)]
            re += r * tc - i * ts
            im += r * ts + i * tc
        re_ref[:, cols] = re
        im_ref[:, cols] = im
    re, im = re_ref[...], im_ref[...]
    power = re * re + im * im
    sums = {}
    for place_of, r in enumerate(CLASSES):
        total = power[:, QUARTER * place_of : QUARTER * (place_of + 1)]
        for step in (1, 2, 4, 8):
            total = total + pltpu.roll(total, QUARTER - step, 1)
        sums[r] = total
    later = {r: pltpu.roll(sums[r], QUARTER - 1, 1) for r in range(3)}
    col = lax.broadcasted_iota(jnp.int32, (CH, QUARTER), 1)
    edge = WIN // 8
    whole = sums[0] + sums[1] + sums[2] + sums[3]
    first, final = whole[:, :1], whole[:, QUARTER - 2 * edge : QUARTER - 2 * edge + 1]
    bands = []
    for r in CLASSES:
        total = sum(later[n] if n < r else sums[n] for n in range(4))
        total = pltpu.roll(total, edge, 1)
        total = jnp.where(col < edge, first, total)
        bands.append(jnp.where(col >= QUARTER - edge, final, total))
    inverse = lax.rsqrt(jnp.concatenate(bands, axis=1) * (1.0 / WIN) + EPS)
    place = (lax.broadcasted_iota(jnp.int32, (CH, CH), 0) == slot_ref[...]).astype(F32).astype(BF16)
    re = dot(place, (re * inverse).astype(BF16))
    im = dot(place, (im * inverse).astype(BF16))
    for n in range(CHUNKS):
        cols = slice(BINS * n, BINS * (n + 1))
        panel_ref[n] = jnp.concatenate([re[:, cols], im[:, cols]], axis=0).astype(BF16)


def whole_bins(panel):
    wide = panel.astype(F32)
    return (
        jnp.concatenate([wide[n, :CH] for n in range(CHUNKS)], axis=1),
        jnp.concatenate([wide[n, CH:] for n in range(CHUNKS)], axis=1),
    )


def correlate_kernel(own_ref, their_ref, lag_hbm, turn_ref, out_ref, lag_ref, turned_ref, cre_ref, cim_ref, load_sem):
    first = (pl.program_id(0) == 0) & (pl.program_id(1) == 0)
    loads = []
    for n in range(2):
        for q in range(4):
            at = (n, pl.ds(QUARTER * q, QUARTER), pl.ds(0, LAG // 2 if q < 2 else LAG))
            loads.append(pltpu.make_async_copy(lag_hbm.at[at], lag_ref.at[at], load_sem.at[4 * n + q]))

    @pl.when(first)
    def _():
        for load in loads:
            load.start()
        own_re, own_im = whole_bins(own_ref[...])
        tr, ti = turn_ref[0:1, :], turn_ref[1:2, :]
        turned_ref[0] = own_re * tr - own_im * ti
        turned_ref[1] = own_re * ti + own_im * tr
        for load in loads:
            load.wait()

    br, bi = whole_bins(their_ref[0])
    at = pl.ds(pl.multiple_of(pl.program_id(1) * OWN_STEP, OWN_STEP), OWN_STEP)
    ar, ai = turned_ref[0, at, :], turned_ref[1, at, :]
    for i in range(0, OWN_STEP, 2):
        res, ims = [], []
        for k in (i, i + 1):
            r, m = ar[k : k + 1], ai[k : k + 1]
            res.append(r * br + m * bi)
            ims.append(m * br - r * bi)
        rows = slice(CH * i, CH * (i + 2))
        cre_ref[rows, :] = jnp.concatenate(res, axis=0).astype(BF16)
        cim_ref[rows, :] = jnp.concatenate(ims, axis=0).astype(BF16)
    lag_rows(cre_ref, cim_ref, lag_ref, out_ref)


def lag_rows(cre_ref, cim_ref, lag_ref, out_ref):
    quarters = slice(0, QUARTER), slice(QUARTER, 2 * QUARTER), slice(2 * QUARTER, NBIN)
    backwards = 127 - lax.broadcasted_iota(jnp.int32, (OWN_STEP * CH, 128), 1)

    def mirror(value, low):
        for n in range(width // 128):
            piece = jnp.take_along_axis(value[:, 128 * n : 128 * (n + 1)], backwards, axis=1, mode="promise_in_bounds")
            yield slice(low + width - 128 * (n + 1), low + width - 128 * n), piece

    width = 256
    half = LAG // 2
    for n in range(half // width):
        near = slice(width * n, width * (n + 1))
        far = slice(LAG - width * (n + 1), LAG - width * n)
        even = [dot(cre_ref[:, rows], lag_ref[0, rows, near]) for rows in quarters[:2]]
        odd = [dot(cim_ref[:, rows], lag_ref[1, rows, near]) for rows in quarters[:2]]
        even_near = even[0] + even[1] + dot(cre_ref[:, quarters[2]], lag_ref[0, quarters[2], near])
        odd_near = odd[0] + odd[1] + dot(cim_ref[:, quarters[2]], lag_ref[1, quarters[2], near])
        out_ref[:, LAG + width * n : LAG + width * (n + 1)] = (even_near + odd_near).astype(BF16)
        for cols, piece in mirror(even_near - odd_near, LAG - width * (n + 1)):
            out_ref[:, cols] = piece.astype(BF16)
        even_far, odd_far = even[0] - even[1], odd[1] - odd[0]
        even_rest = dot(cre_ref[:, quarters[2]], lag_ref[0, quarters[2], far])
        odd_rest = dot(cim_ref[:, quarters[2]], lag_ref[1, quarters[2], far])
        rest = even_rest + odd_rest
        for cols, piece in mirror(even_far + odd_far, 0):
            out_ref[:, 2 * LAG - width * (n + 1) + cols.start : 2 * LAG - width * (n + 1) + cols.stop] = (piece + rest[:, cols]).astype(BF16)
        straight = even_far - odd_far
        for cols, piece in mirror(even_rest - odd_rest, 0):
            out_ref[:, width * n + cols.start : width * n + cols.stop] = (piece + straight[:, cols]).astype(BF16)


MESH_ID = pl.DeviceIdType.MESH


def choose(first, a, b):
    return jnp.where(first, a.astype(F32), b.astype(F32)).astype(BF16)


def exchange_kernel(pairings_ref, subset_ref, raw_hbm, taps_hbm, slot_hbm, tables_hbm, shift_hbm, panel_ref, theirs_ref,
                    raw_ref, taps_ref, slot_ref, tables_ref, shift_ref, filter_ref, dh_ref, dl_ref, re_ref, im_ref, load_sem,
                    meta, peers, flat, pair, *rest):
    shared, single = rest[:CHUNKS], rest[CHUNKS : CHUNKS * (1 + ROUNDS)]
    send, recv, local = rest[CHUNKS * (1 + ROUNDS) :]
    g, m = lax.axis_index("group"), lax.axis_index("member")
    z, h = g // 2, g % 2
    l, x, c = m // 8, (m // 2) % 4, m % 2
    k = x * 2 + c

    def at(dz=0, dh=0, dl=0, dx=0, dc=0):
        group = lax.rem(z + dz, 4) * 2 + lax.rem(h + dh, 2)
        member = lax.rem(l + dl, 2) * 8 + lax.rem(x + dx, 4) * 2 + lax.rem(c + dc, 2)
        return group, member

    along_x = [at(dx=d) for d in (2, 1, 3)]
    along_z = [at(dz=d) for d in (2, 1, 3)]
    core, low, high = at(dc=1), at(dl=1), at(dh=1)
    started = []

    def put(src, dst, where):
        n = len(started)
        copy = pltpu.make_async_remote_copy(
            src_ref=src, dst_ref=dst, send_sem=send.at[n], recv_sem=recv.at[n], device_id=where, device_id_type=MESH_ID
        )
        copy.start()
        started.append(copy)
        return copy

    barrier = pltpu.get_barrier_semaphore()
    everyone = along_x + along_z + [core, low, high]
    for where in everyone:
        pl.semaphore_signal(barrier, inc=1, device_id=where, device_id_type=MESH_ID)

    loads = []
    moves = ((raw_hbm, raw_ref), (taps_hbm, taps_ref), (slot_hbm, slot_ref), (tables_hbm, tables_ref), (shift_hbm, shift_ref))
    for n, (src, dst) in enumerate(moves):
        loads.append(pltpu.make_async_copy(src, dst, load_sem.at[n]))
        loads[-1].start()
    index = lax.broadcasted_iota(jnp.int32, (8, 128), 0)
    mine = jnp.zeros((8, 128), jnp.int32)
    for r in range(ROUNDS):
        mine = jnp.where(index == r, pairings_ref[r], mine)
        mine = jnp.where(index == ROUNDS + r, subset_ref[r], mine)
    meta[...] = mine
    whiten_block(
        raw_ref, taps_ref, slot_ref, tables_ref, shift_ref, panel_ref, filter_ref, dh_ref, dl_ref, re_ref, im_ref, loads
    )
    pl.semaphore_wait(barrier, len(everyone))

    asks = [put(meta, peers.at[0], low), put(meta, peers.at[1], high)]
    my_pair = [pairings_ref[r] for r in range(ROUNDS)]
    my_sub = [subset_ref[r] for r in range(ROUNDS)]
    in_group = [lax.rem(my_pair[r], 2) == h for r in range(ROUNDS)]
    in_member = [my_sub[r] // 8 == l for r in range(ROUNDS)]
    my_z = [my_pair[r] // 2 for r in range(ROUNDS)]
    my_k = [lax.rem(my_sub[r], 8) for r in range(ROUNDS)]
    even, odd = tuple(range(0, CHUNKS, 2)), tuple(range(1, CHUNKS, 2))
    hers = {}
    moving = {}

    def read_asks():
        for ask in asks:
            ask.wait_recv()
        fetch = pltpu.make_async_copy(peers, flat, local)
        fetch.start()
        fetch.wait()
        for r in range(ROUNDS):
            hers["k", r] = lax.rem(flat[0, ROUNDS + r, 0], 8)
            hers["z", r] = flat[1, r, 0] // 2

    def store(q, r):
        return shared[q] if r < 0 else single[q * ROUNDS + r]

    def by_row(q, r):
        return (q % 2 == 0) == (r < 0)

    def slot(dx):
        return lax.rem(x + dx, 4) * 2 + c

    def gather(q, r):
        room = store(q, r)
        if by_row(q, r):
            own, targets = room.at[k], along_x + [core]
        else:
            own, targets = room.at[z], along_z
        src = own
        if r < 0:
            room[k if by_row(q, r) else z] = panel_ref[q]
            src = panel_ref.at[q]
        moving[q, r] = [put(src, own, where) for where in targets]

    def forward(q, r):
        if by_row(q, r):
            room, copies = store(q, r), moving[q, r]
            for copy, dx in zip(copies[:3], (2, 3, 1)):
                copy.wait_recv()
                got = room.at[slot(dx)]
                copies.append(put(got, got, core))
            del copies[:3]

    def ask_pair(q, stage, r):
        if (q, stage) in moving:
            for copy in moving.pop((q, stage)):
                copy.wait_recv()
        out, into = (0, 1) if stage < 0 else (2, 3)
        row = by_row(q, stage)
        pair[q, r, out] = store(q, stage)[hers["k" if row else "z", r]]
        moving[q, stage, r] = put(pair.at[q, r, out], pair.at[q, r, into], low if row else high)

    def chosen(q, stage, r):
        moving.pop((q, stage, r)).wait_recv()
        into = pair[q, r, 1 if stage < 0 else 3]
        if by_row(q, stage):
            return choose(in_member[r], store(q, stage)[my_k[r]], into)
        return choose(in_group[r], store(q, stage)[my_z[r]], into)

    def regroup(q, r):
        single[q * ROUNDS + r][k if by_row(q, r) else z] = chosen(q, -1, r)
        gather(q, r)

    def finish(q, r):
        theirs_ref[r, q] = chosen(q, r, r)

    for q in range(CHUNKS):
        gather(q, -1)
    read_asks()
    for q in even:
        forward(q, -1)
    for r in range(ROUNDS):
        for q in odd + even:
            ask_pair(q, -1, r)
    for r in range(ROUNDS):
        for q in odd + even:
            regroup(q, r)
    for r in range(ROUNDS):
        for q in odd:
            forward(q, r)
        for q in even + odd:
            ask_pair(q, r, r)
    for r in range(ROUNDS):
        for q in even + odd:
            finish(q, r)
    for copy in started:
        copy.wait_send()


COPIES = 2 + CHUNKS // 2 * 38


def exchange(raw_strain, fir_taps, block_slot, pairings, subset):
    part = (2 * CH, BINS)
    tables, shift = forward_tables()
    return pl.pallas_call(
        exchange_kernel,
        out_shape=(
            jax.ShapeDtypeStruct((CHUNKS,) + part, BF16),
            jax.ShapeDtypeStruct((ROUNDS, CHUNKS) + part, BF16),
        ),
        in_specs=[pl.BlockSpec(memory_space=pltpu.SMEM)] * 2 + [pl.BlockSpec(memory_space=pltpu.HBM)] * 5,
        out_specs=(pl.BlockSpec(memory_space=pltpu.VMEM), pl.BlockSpec(memory_space=pltpu.VMEM)),
        scratch_shapes=[
            pltpu.VMEM((CH, RAW), F32),
            pltpu.VMEM((1, TAPS), F32),
            pltpu.VMEM((1, CH), jnp.int32),
            pltpu.VMEM((2, PIECE, 2 * NBIN), BF16),
            pltpu.VMEM((2, PIECES, NBIN), F32),
            pltpu.VMEM((1, SPAN), F32),
            pltpu.VMEM((PIECES * CH, PIECE), BF16),
            pltpu.VMEM((PIECES * CH, PIECE), BF16),
            pltpu.VMEM((CH, NBIN), F32),
            pltpu.VMEM((CH, NBIN), F32),
            pltpu.SemaphoreType.DMA((5,)),
            pltpu.VMEM((8, 128), jnp.int32),
            pltpu.VMEM((2, 8, 128), jnp.int32),
            pltpu.SMEM((2, 8, 128), jnp.int32),
            pltpu.VMEM((CHUNKS, ROUNDS, 4) + part, BF16),
        ]
        + [pltpu.VMEM((8 if q % 2 == 0 else 4,) + part, BF16) for q in range(CHUNKS)]
        + [pltpu.VMEM((4 if q % 2 == 0 else 8,) + part, BF16) for q in range(CHUNKS) for r in range(ROUNDS)]
        + [
            pltpu.SemaphoreType.DMA((COPIES,)),
            pltpu.SemaphoreType.DMA((COPIES,)),
            pltpu.SemaphoreType.DMA,
        ],
        compiler_params=pltpu.CompilerParams(collective_id=1, has_side_effects=True, vmem_limit_bytes=GRANT),
        name="exchange",
    )(pairings, subset, raw_strain, fir_taps.reshape(1, TAPS), block_slot.reshape(1, CH), tables, shift)


def correlate(own, theirs):
    lags, turn = lag_tables()
    rows = OWN_STEP * CH
    steps = CH // OWN_STEP
    whole = lambda r, i: (0, 0)
    return pl.pallas_call(
        correlate_kernel,
        grid=(ROUNDS, steps),
        out_shape=jax.ShapeDtypeStruct((ROUNDS * CH * CH, 2 * LAG), BF16),
        in_specs=[
            pl.BlockSpec((CHUNKS, 2 * CH, BINS), lambda r, i: (0, 0, 0)),
            pl.BlockSpec((1, CHUNKS, 2 * CH, BINS), lambda r, i: (r, 0, 0, 0)),
            pl.BlockSpec(memory_space=pltpu.HBM),
            pl.BlockSpec((2, NBIN), whole),
        ],
        out_specs=pl.BlockSpec((rows, 2 * LAG), lambda r, i: (r * steps + i, 0)),
        scratch_shapes=[
            pltpu.VMEM((2, NBIN, LAG), BF16),
            pltpu.VMEM((2, CH, NBIN), F32),
            pltpu.VMEM((rows, NBIN), BF16),
            pltpu.VMEM((rows, NBIN), BF16),
            pltpu.SemaphoreType.DMA((8,)),
        ],
        compiler_params=pltpu.CompilerParams(vmem_limit_bytes=GRANT),
    )(own, theirs, lags, turn)


def per_device(raw_strain, fir_taps, block_slot, pairings, pair_subset):
    panel, theirs = exchange(
        raw_strain, fir_taps, block_slot, pairings.reshape(ROUNDS), pair_subset.reshape(ROUNDS)
    )
    result = correlate(panel, theirs)
    return result.reshape(ROUNDS, KSUB, CH, CH, 2 * LAG)


def solution(mesh):
    in_specs = (
        P(("group", "member"), None),
        P(),
        P(("group", "member")),
        P(None, "group"),
        P(None, "member", None),
    )
    out_specs = P(None, None, ("group", "member"), None, None)
    return jax.shard_map(
        per_device, mesh=mesh, in_specs=in_specs, out_specs=out_specs, check_vma=False
    )
```

```python
import functools
import math

import jax
import jax.numpy as jnp
import ml_dtypes
import numpy as np
from jax import lax
from jax.experimental import pallas as pl
from jax.experimental.pallas import tpu as pltpu
from jax.sharding import PartitionSpec as P

SEG = 2048
TAPS = 64
NFFT = 4096
F0 = 24
NBIN = 1024
WIN = 64
LAG = 1024
ROUNDS = 2
KSUB = 1
CH = 40
RAW = 4160
EPS = 1e-06

PIECE = 256
PIECES = SEG // PIECE
SPAN = 640
OWN_STEP = 8
MIB = 1 << 20
CLASSES = (0, 2, 1, 3)
QUARTER = NBIN // 4
GRANT = 63 * MIB
CHUNKS = 4
BINS = NBIN // CHUNKS
BF16 = jnp.bfloat16
F32 = jnp.float32


def split_bf16(table):
    high = table.astype(ml_dtypes.bfloat16)
    low = (table - high.astype(np.float64)).astype(ml_dtypes.bfloat16)
    return high, low


def bin_order():
    return np.concatenate([np.arange(r, NBIN, 4) for r in CLASSES])


def forward_tables():
    bins = F0 + bin_order()
    phases = np.arange(PIECE)[:, None] * bins[None, :] % NFFT * (2.0 * math.pi / NFFT)
    high, low = split_bf16(np.concatenate([np.cos(phases), -np.sin(phases)], axis=1))
    shift = np.arange(PIECES)[:, None] * PIECE * bins[None, :] % NFFT * (2.0 * math.pi / NFFT)
    return np.stack([high, low]), np.stack([np.cos(shift), -np.sin(shift)]).astype(np.float32)


def lag_tables():
    bins = F0 + bin_order()
    phases = bins[:, None] * (2 * np.arange(LAG) + 1)[None, :] % (2 * NFFT) * (math.pi / NFFT)
    scale = 1.0 / math.sqrt(NBIN)
    cosine = (np.cos(phases) * scale).astype(ml_dtypes.bfloat16)
    sine = (-np.sin(phases) * scale).astype(ml_dtypes.bfloat16)
    half = bins * (math.pi / NFFT)
    turn = np.stack([np.cos(half), -np.sin(half)]).astype(np.float32)
    return np.stack([cosine, sine]), turn


def dot(a, b):
    return jnp.dot(a, b, preferred_element_type=F32)


def parts(x):
    high = x.astype(BF16)
    return high, (x - high.astype(F32)).astype(BF16)


def whiten_block(raw_ref, taps_ref, slot_ref, tables_ref, shift_ref, panel_ref, filter_ref, dh_ref, dl_ref, re_ref, im_ref, loads):
    for load in loads[:3]:
        load.wait()
    filter_ref[...] = jnp.zeros((1, SPAN), F32)
    filter_ref[:, :TAPS] = taps_ref[...]
    filter_rows = pltpu.roll(jnp.broadcast_to(filter_ref[...], (PIECE, SPAN)), 0, 1, stride=2, stride_axis=0)
    pieces = [raw_ref[:, 2 * PIECE * b : 2 * PIECE * b + SPAN] for b in range(PIECES - 1)]
    last = raw_ref[:, 2 * PIECE * (PIECES - 1) :]
    pieces.append(jnp.concatenate([last, jnp.zeros((CH, SPAN - last.shape[1]), F32)], axis=1))
    xh, xl = parts(jnp.concatenate(pieces, axis=0))
    fh, fl = parts(filter_rows)
    contract = functools.partial(
        lax.dot_general, dimension_numbers=(((1,), (1,)), ((), ())), preferred_element_type=F32
    )
    dh, dl = parts(contract(xh, fh) + contract(xl, fh) + contract(xh, fl))
    dh_ref[...] = dh
    dl_ref[...] = dl
    for load in loads[3:]:
        load.wait()
    width = 256
    for n in range(NBIN // width):
        cols = slice(width * n, width * (n + 1))
        both = []
        for base in (0, NBIN):
            at = slice(base + width * n, base + width * (n + 1))
            wide = dh_ref[...]
            both.append(
                dot(wide, tables_ref[0, :, at]) + dot(dl_ref[...], tables_ref[0, :, at]) + dot(wide, tables_ref[1, :, at])
            )
        yr, yi = both
        re = jnp.zeros((CH, width), F32)
        im = jnp.zeros((CH, width), F32)
        for b in range(PIECES):
            tc = shift_ref[0, b : b + 1, cols]
            ts = shift_ref[1, b : b + 1, cols]
            r, i = yr[CH * b : CH * (b + 1)], yi[CH * b : CH * (b + 1)]
            re += r * tc - i * ts
            im += r * ts + i * tc
        re_ref[:, cols] = re
        im_ref[:, cols] = im
    re, im = re_ref[...], im_ref[...]
    power = re * re + im * im
    sums = {}
    for place_of, r in enumerate(CLASSES):
        total = power[:, QUARTER * place_of : QUARTER * (place_of + 1)]
        for step in (1, 2, 4, 8):
            total = total + pltpu.roll(total, QUARTER - step, 1)
        sums[r] = total
    later = {r: pltpu.roll(sums[r], QUARTER - 1, 1) for r in range(3)}
    col = lax.broadcasted_iota(jnp.int32, (CH, QUARTER), 1)
    edge = WIN // 8
    whole = sums[0] + sums[1] + sums[2] + sums[3]
    first, final = whole[:, :1], whole[:, QUARTER - 2 * edge : QUARTER - 2 * edge + 1]
    bands = []
    for r in CLASSES:
        total = sum(later[n] if n < r else sums[n] for n in range(4))
        total = pltpu.roll(total, edge, 1)
        total = jnp.where(col < edge, first, total)
        bands.append(jnp.where(col >= QUARTER - edge, final, total))
    inverse = lax.rsqrt(jnp.concatenate(bands, axis=1) * (1.0 / WIN) + EPS)
    place = (lax.broadcasted_iota(jnp.int32, (CH, CH), 0) == slot_ref[...]).astype(F32).astype(BF16)
    re = dot(place, (re * inverse).astype(BF16))
    im = dot(place, (im * inverse).astype(BF16))
    for n in range(CHUNKS):
        cols = slice(BINS * n, BINS * (n + 1))
        panel_ref[n] = jnp.concatenate([re[:, cols], im[:, cols]], axis=0).astype(BF16)


def whole_bins(panel):
    wide = panel.astype(F32)
    return (
        jnp.concatenate([wide[n, :CH] for n in range(CHUNKS)], axis=1),
        jnp.concatenate([wide[n, CH:] for n in range(CHUNKS)], axis=1),
    )


def correlate_kernel(own_ref, their_ref, lag_hbm, turn_ref, out_ref, lag_ref, turned_ref, cre_ref, cim_ref, load_sem):
    first = (pl.program_id(0) == 0) & (pl.program_id(1) == 0)
    loads = []
    for n in range(2):
        for q in range(4):
            at = (n, pl.ds(QUARTER * q, QUARTER), pl.ds(0, LAG // 2 if q < 2 else LAG))
            loads.append(pltpu.make_async_copy(lag_hbm.at[at], lag_ref.at[at], load_sem.at[4 * n + q]))

    @pl.when(first)
    def _():
        for load in loads:
            load.start()
        own_re, own_im = whole_bins(own_ref[...])
        tr, ti = turn_ref[0:1, :], turn_ref[1:2, :]
        turned_ref[0] = own_re * tr - own_im * ti
        turned_ref[1] = own_re * ti + own_im * tr
        for load in loads:
            load.wait()

    br, bi = whole_bins(their_ref[0])
    at = pl.ds(pl.multiple_of(pl.program_id(1) * OWN_STEP, OWN_STEP), OWN_STEP)
    ar, ai = turned_ref[0, at, :], turned_ref[1, at, :]
    for i in range(0, OWN_STEP, 2):
        res, ims = [], []
        for k in (i, i + 1):
            r, m = ar[k : k + 1], ai[k : k + 1]
            res.append(r * br + m * bi)
            ims.append(m * br - r * bi)
        rows = slice(CH * i, CH * (i + 2))
        cre_ref[rows, :] = jnp.concatenate(res, axis=0).astype(BF16)
        cim_ref[rows, :] = jnp.concatenate(ims, axis=0).astype(BF16)
    lag_rows(cre_ref, cim_ref, lag_ref, out_ref)


def lag_rows(cre_ref, cim_ref, lag_ref, out_ref):
    quarters = slice(0, QUARTER), slice(QUARTER, 2 * QUARTER), slice(2 * QUARTER, NBIN)
    backwards = 127 - lax.broadcasted_iota(jnp.int32, (OWN_STEP * CH, 128), 1)

    def mirror(value, low):
        for n in range(width // 128):
            piece = jnp.take_along_axis(value[:, 128 * n : 128 * (n + 1)], backwards, axis=1, mode="promise_in_bounds")
            yield slice(low + width - 128 * (n + 1), low + width - 128 * n), piece

    width = 256
    half = LAG // 2
    for n in range(half // width):
        near = slice(width * n, width * (n + 1))
        far = slice(LAG - width * (n + 1), LAG - width * n)
        even = [dot(cre_ref[:, rows], lag_ref[0, rows, near]) for rows in quarters[:2]]
        odd = [dot(cim_ref[:, rows], lag_ref[1, rows, near]) for rows in quarters[:2]]
        even_near = even[0] + even[1] + dot(cre_ref[:, quarters[2]], lag_ref[0, quarters[2], near])
        odd_near = odd[0] + odd[1] + dot(cim_ref[:, quarters[2]], lag_ref[1, quarters[2], near])
        out_ref[:, LAG + width * n : LAG + width * (n + 1)] = (even_near + odd_near).astype(BF16)
        for cols, piece in mirror(even_near - odd_near, LAG - width * (n + 1)):
            out_ref[:, cols] = piece.astype(BF16)
        even_far, odd_far = even[0] - even[1], odd[1] - odd[0]
        even_rest = dot(cre_ref[:, quarters[2]], lag_ref[0, quarters[2], far])
        odd_rest = dot(cim_ref[:, quarters[2]], lag_ref[1, quarters[2], far])
        rest = even_rest + odd_rest
        for cols, piece in mirror(even_far + odd_far, 0):
            out_ref[:, 2 * LAG - width * (n + 1) + cols.start : 2 * LAG - width * (n + 1) + cols.stop] = (piece + rest[:, cols]).astype(BF16)
        straight = even_far - odd_far
        for cols, piece in mirror(even_rest - odd_rest, 0):
            out_ref[:, width * n + cols.start : width * n + cols.stop] = (piece + straight[:, cols]).astype(BF16)


MESH_ID = pl.DeviceIdType.MESH


def choose(first, a, b):
    return jnp.where(first, a.astype(F32), b.astype(F32)).astype(BF16)


def exchange_kernel(pairings_ref, subset_ref, raw_hbm, taps_hbm, slot_hbm, tables_hbm, shift_hbm, panel_ref, theirs_ref,
                    raw_ref, taps_ref, slot_ref, tables_ref, shift_ref, filter_ref, dh_ref, dl_ref, re_ref, im_ref, load_sem,
                    meta, peers, flat, pair, *rest):
    shared, single = rest[:CHUNKS], rest[CHUNKS : CHUNKS * (1 + ROUNDS)]
    send, recv, local = rest[CHUNKS * (1 + ROUNDS) :]
    g, m = lax.axis_index("group"), lax.axis_index("member")
    z, h = g // 2, g % 2
    l, x, c = m // 8, (m // 2) % 4, m % 2
    k = x * 2 + c

    def at(dz=0, dh=0, dl=0, dx=0, dc=0):
        group = lax.rem(z + dz, 4) * 2 + lax.rem(h + dh, 2)
        member = lax.rem(l + dl, 2) * 8 + lax.rem(x + dx, 4) * 2 + lax.rem(c + dc, 2)
        return group, member

    along_x = [at(dx=d) for d in (2, 1, 3)]
    along_z = [at(dz=d) for d in (2, 1, 3)]
    core, low, high = at(dc=1), at(dl=1), at(dh=1)
    started = []

    def put(src, dst, where):
        n = len(started)
        copy = pltpu.make_async_remote_copy(
            src_ref=src, dst_ref=dst, send_sem=send.at[n], recv_sem=recv.at[n], device_id=where, device_id_type=MESH_ID
        )
        copy.start()
        started.append(copy)
        return copy

    barrier = pltpu.get_barrier_semaphore()
    everyone = along_x + along_z + [core, low, high]
    for where in everyone:
        pl.semaphore_signal(barrier, inc=1, device_id=where, device_id_type=MESH_ID)

    loads = []
    moves = ((raw_hbm, raw_ref), (taps_hbm, taps_ref), (slot_hbm, slot_ref), (tables_hbm, tables_ref), (shift_hbm, shift_ref))
    for n, (src, dst) in enumerate(moves):
        loads.append(pltpu.make_async_copy(src, dst, load_sem.at[n]))
        loads[-1].start()
    index = lax.broadcasted_iota(jnp.int32, (8, 128), 0)
    mine = jnp.zeros((8, 128), jnp.int32)
    for r in range(ROUNDS):
        mine = jnp.where(index == r, pairings_ref[r], mine)
        mine = jnp.where(index == ROUNDS + r, subset_ref[r], mine)
    meta[...] = mine
    whiten_block(
        raw_ref, taps_ref, slot_ref, tables_ref, shift_ref, panel_ref, filter_ref, dh_ref, dl_ref, re_ref, im_ref, loads
    )
    pl.semaphore_wait(barrier, len(everyone))

    asks = [put(meta, peers.at[0], low), put(meta, peers.at[1], high)]
    my_pair = [pairings_ref[r] for r in range(ROUNDS)]
    my_sub = [subset_ref[r] for r in range(ROUNDS)]
    in_group = [lax.rem(my_pair[r], 2) == h for r in range(ROUNDS)]
    in_member = [my_sub[r] // 8 == l for r in range(ROUNDS)]
    my_z = [my_pair[r] // 2 for r in range(ROUNDS)]
    my_k = [lax.rem(my_sub[r], 8) for r in range(ROUNDS)]
    even, odd = tuple(range(0, CHUNKS, 2)), tuple(range(1, CHUNKS, 2))
    hers = {}
    moving = {}

    def read_asks():
        for ask in asks:
            ask.wait_recv()
        fetch = pltpu.make_async_copy(peers, flat, local)
        fetch.start()
        fetch.wait()
        for r in range(ROUNDS):
            hers["k", r] = lax.rem(flat[0, ROUNDS + r, 0], 8)
            hers["z", r] = flat[1, r, 0] // 2

    def store(q, r):
        return shared[q] if r < 0 else single[q * ROUNDS + r]

    def by_row(q, r):
        return (q % 2 == 0) == (r < 0)

    def slot(dx):
        return lax.rem(x + dx, 4) * 2 + c

    def gather(q, r):
        room = store(q, r)
        if by_row(q, r):
            own, targets = room.at[k], along_x + [core]
        else:
            own, targets = room.at[z], along_z
        src = own
        if r < 0:
            room[k if by_row(q, r) else z] = panel_ref[q]
            src = panel_ref.at[q]
        moving[q, r] = [put(src, own, where) for where in targets]

    def forward(q, r):
        if by_row(q, r):
            room, copies = store(q, r), moving[q, r]
            for copy, dx in zip(copies[:3], (2, 3, 1)):
                copy.wait_recv()
                got = room.at[slot(dx)]
                copies.append(put(got, got, core))
            del copies[:3]

    def ask_pair(q, stage, r):
        if (q, stage) in moving:
            for copy in moving.pop((q, stage)):
                copy.wait_recv()
        out, into = (0, 1) if stage < 0 else (2, 3)
        row = by_row(q, stage)
        pair[q, r, out] = store(q, stage)[hers["k" if row else "z", r]]
        moving[q, stage, r] = put(pair.at[q, r, out], pair.at[q, r, into], low if row else high)

    def chosen(q, stage, r):
        moving.pop((q, stage, r)).wait_recv()
        into = pair[q, r, 1 if stage < 0 else 3]
        if by_row(q, stage):
            return choose(in_member[r], store(q, stage)[my_k[r]], into)
        return choose(in_group[r], store(q, stage)[my_z[r]], into)

    def regroup(q, r):
        single[q * ROUNDS + r][k if by_row(q, r) else z] = chosen(q, -1, r)
        gather(q, r)

    def finish(q, r):
        theirs_ref[r, q] = chosen(q, r, r)

    for q in range(CHUNKS):
        gather(q, -1)
    for q in even:
        forward(q, -1)
    read_asks()
    for r in range(ROUNDS):
        for q in odd + even:
            ask_pair(q, -1, r)
    for r in range(ROUNDS):
        for q in odd + even:
            regroup(q, r)
    for r in range(ROUNDS):
        for q in odd:
            forward(q, r)
        for q in even + odd:
            ask_pair(q, r, r)
    for r in range(ROUNDS):
        for q in even + odd:
            finish(q, r)
    for copy in started:
        copy.wait_send()


COPIES = 2 + CHUNKS // 2 * 38


def exchange(raw_strain, fir_taps, block_slot, pairings, subset):
    part = (2 * CH, BINS)
    tables, shift = forward_tables()
    return pl.pallas_call(
        exchange_kernel,
        out_shape=(
            jax.ShapeDtypeStruct((CHUNKS,) + part, BF16),
            jax.ShapeDtypeStruct((ROUNDS, CHUNKS) + part, BF16),
        ),
        in_specs=[pl.BlockSpec(memory_space=pltpu.SMEM)] * 2 + [pl.BlockSpec(memory_space=pltpu.HBM)] * 5,
        out_specs=(pl.BlockSpec(memory_space=pltpu.VMEM), pl.BlockSpec(memory_space=pltpu.VMEM)),
        scratch_shapes=[
            pltpu.VMEM((CH, RAW), F32),
            pltpu.VMEM((1, TAPS), F32),
            pltpu.VMEM((1, CH), jnp.int32),
            pltpu.VMEM((2, PIECE, 2 * NBIN), BF16),
            pltpu.VMEM((2, PIECES, NBIN), F32),
            pltpu.VMEM((1, SPAN), F32),
            pltpu.VMEM((PIECES * CH, PIECE), BF16),
            pltpu.VMEM((PIECES * CH, PIECE), BF16),
            pltpu.VMEM((CH, NBIN), F32),
            pltpu.VMEM((CH, NBIN), F32),
            pltpu.SemaphoreType.DMA((5,)),
            pltpu.VMEM((8, 128), jnp.int32),
            pltpu.VMEM((2, 8, 128), jnp.int32),
            pltpu.SMEM((2, 8, 128), jnp.int32),
            pltpu.VMEM((CHUNKS, ROUNDS, 4) + part, BF16),
        ]
        + [pltpu.VMEM((8 if q % 2 == 0 else 4,) + part, BF16) for q in range(CHUNKS)]
        + [pltpu.VMEM((4 if q % 2 == 0 else 8,) + part, BF16) for q in range(CHUNKS) for r in range(ROUNDS)]
        + [
            pltpu.SemaphoreType.DMA((COPIES,)),
            pltpu.SemaphoreType.DMA((COPIES,)),
            pltpu.SemaphoreType.DMA,
        ],
        compiler_params=pltpu.CompilerParams(collective_id=1, has_side_effects=True, vmem_limit_bytes=GRANT),
        name="exchange",
    )(pairings, subset, raw_strain, fir_taps.reshape(1, TAPS), block_slot.reshape(1, CH), tables, shift)


def correlate(own, theirs):
    lags, turn = lag_tables()
    rows = OWN_STEP * CH
    steps = CH // OWN_STEP
    whole = lambda r, i: (0, 0)
    return pl.pallas_call(
        correlate_kernel,
        grid=(ROUNDS, steps),
        out_shape=jax.ShapeDtypeStruct((ROUNDS * CH * CH, 2 * LAG), BF16),
        in_specs=[
            pl.BlockSpec((CHUNKS, 2 * CH, BINS), lambda r, i: (0, 0, 0)),
            pl.BlockSpec((1, CHUNKS, 2 * CH, BINS), lambda r, i: (r, 0, 0, 0)),
            pl.BlockSpec(memory_space=pltpu.HBM),
            pl.BlockSpec((2, NBIN), whole),
        ],
        out_specs=pl.BlockSpec((rows, 2 * LAG), lambda r, i: (r * steps + i, 0)),
        scratch_shapes=[
            pltpu.VMEM((2, NBIN, LAG), BF16),
            pltpu.VMEM((2, CH, NBIN), F32),
            pltpu.VMEM((rows, NBIN), BF16),
            pltpu.VMEM((rows, NBIN), BF16),
            pltpu.SemaphoreType.DMA((8,)),
        ],
        compiler_params=pltpu.CompilerParams(vmem_limit_bytes=GRANT),
    )(own, theirs, lags, turn)


def per_device(raw_strain, fir_taps, block_slot, pairings, pair_subset):
    panel, theirs = exchange(
        raw_strain, fir_taps, block_slot, pairings.reshape(ROUNDS), pair_subset.reshape(ROUNDS)
    )
    result = correlate(panel, theirs)
    return result.reshape(ROUNDS, KSUB, CH, CH, 2 * LAG)


def solution(mesh):
    in_specs = (
        P(("group", "member"), None),
        P(),
        P(("group", "member")),
        P(None, "group"),
        P(None, "member", None),
    )
    out_specs = P(None, None, ("group", "member"), None, None)
    return jax.shard_map(
        per_device, mesh=mesh, in_specs=in_specs, out_specs=out_specs, check_vma=False
    )
```
